256 devices in a mesh: patch: 64 (over x, z_lo, y, core), tp: 4 (over z_hi).
Axes of the slice: x: 4, y: 4, z: 8 (z_hi: 4, z_lo: 2; z = z_hi * 2 + z_lo), core: 2. Of those that a mesh axis runs over, the one named last changes fastest.
Arguments:
- activations: bfloat16 [2, 4096, 4096], P(None, 'patch', 'tp'), may hold values from -3000 to 3000
- mod_shift: bfloat16 [2, 4096], P(None, 'tp'), may hold values from -3 to 3
- mod_scale: bfloat16 [2, 4096], P(None, 'tp'), may hold values from -3 to 3
- w_query: bfloat16 [4096, 2048], P(None, 'tp'), may hold values from -0.09375 to 0.09375
- w_key: bfloat16 [4096, 2048], P(None, 'tp'), may hold values from -0.09375 to 0.09375
- w_value: bfloat16 [4096, 2048], P(None, 'tp'), may hold values from -0.09375 to 0.09375
- query_gain: float32 [128], replicated, may hold values from 1 to 2.5
- key_gain: float32 [128], replicated, may hold values from 1 to 2.5
- stale_keys: bfloat16 [2, 4096, 2048], P(None, 'patch', 'tp'), may hold values from -200 to 200
- stale_values: bfloat16 [2, 4096, 2048], P(None, 'patch', 'tp'), may hold values from -6 to 6
Outputs:
- attended: bfloat16 [2, 4096, 2048], P(None, 'patch', 'tp')
- fresh_keys: bfloat16 [2, 4096, 2048], P(None, 'patch', 'tp')
- fresh_values: bfloat16 [2, 4096, 2048], P(None, 'patch', 'tp')
The draws below stay inside these ranges and needn't reach their ends.
All inputs are finite; a program needn't handle non-finite values.
Results may differ from the reference program's by a relative error of at most 0.022.
Values may be sent and summed in bfloat16 or wider, within the bound.
No kernel may reach another device: no remote copies, remote signals or barrier semaphores. Data moves between devices by JAX's collectives and lax.ppermute only.
A program may use at most 128 MiB of HBM per device.

```python
import math
import jax
import jax.numpy as jnp
from jax import lax

D = 4096
HEADS = 16
HEAD_DIM = 128
IMAGES = 2
TOK_DEV = 64
TOKENS = 4096
N_PATCH = 64


def draw_activations(key, part):
    key = jax.random.fold_in(key, 11)
    first = jax.random.fold_in(key, 0)
    ramp = jnp.arange(D, dtype=jnp.float32) / D
    drawn = jnp.clip(jax.random.normal(first, (IMAGES, TOKENS, D), jnp.float32), -6.0, 6.0) * jnp.exp(ramp * math.log(3.0))
    return drawn.astype(jnp.bfloat16)


def draw_stale_keys(key, part):
    key = jax.random.fold_in(key, 23)
    first = jax.random.fold_in(key, 0)
    features = HEADS * HEAD_DIM
    drawn = jnp.clip(jax.random.normal(first, (IMAGES, TOKENS, features), jnp.float32), -6.0, 6.0) * 1.6
    return drawn.astype(jnp.bfloat16)


def block_levels(rng, shape, cuts, smallest, top_value):
    factor_of = 1.0
    for dim, shards_of in cuts:
        steps = jax.random.uniform(jax.random.fold_in(jax.random.fold_in(rng, 6), dim), (shards_of,), jnp.float32, smallest / len(cuts), top_value / len(cuts))
        factor_of = factor_of * jnp.repeat(jnp.exp(steps), shape[dim] // shards_of).reshape((-1,) + (1,) * (len(shape) - 1 - dim))
    return factor_of


def normal_values(own_key, shape, width, bound, pieces=(), held_as=jnp.bfloat16):
    level = block_levels(own_key, shape, pieces, -0.22, 0.18) if pieces else 1.0
    entries = jax.random.normal(own_key, shape, jnp.float32) * width * level
    return jnp.minimum(jnp.maximum(entries, -bound), bound).astype(held_as)


def setup_inputs(seed: int = 0) -> dict:
    key_list = jax.random.split(jax.random.key(seed), 11)
    return {
        "activations": draw_activations(jax.random.fold_in(key_list[10], 71), 0),
        "mod_shift": normal_values(key_list[1], (IMAGES, D), 0.5, 3.0, ((1, 4),)),
        "mod_scale": normal_values(key_list[2], (IMAGES, D), 0.5, 3.0, ((1, 4),)),
        "w_query": normal_values(key_list[3], (D, HEADS * HEAD_DIM), D ** -0.5, 0.09375, ((1, 4),)),
        "w_key": normal_values(key_list[4], (D, HEADS * HEAD_DIM), D ** -0.5, 0.09375, ((1, 4),)),
        "w_value": normal_values(key_list[5], (D, HEADS * HEAD_DIM), D ** -0.5, 0.09375, ((1, 4),)),
        "query_gain": jnp.clip(jnp.exp(jax.random.uniform(key_list[6], (HEAD_DIM,), jnp.float32, math.log(1.0), math.log(2.5))), 1.0, 2.5),
        "key_gain": jnp.clip(jnp.exp(jax.random.uniform(key_list[7], (HEAD_DIM,), jnp.float32, math.log(1.0), math.log(2.5))), 1.0, 2.5),
        "stale_keys": draw_stale_keys(jax.random.fold_in(key_list[10], 71), 0),
        "stale_values": normal_values(key_list[9], (IMAGES, TOKENS, HEADS * HEAD_DIM), 1.0, 6.0, ((1, 64), (2, 4))),
    }


def modulate(activations, mod_shift, mod_scale):
    values = activations.astype(jnp.float32)
    row_mean = lax.optimization_barrier(jnp.mean(values, axis=-1, keepdims=True))
    centred = values - row_mean
    row_var = lax.optimization_barrier(jnp.mean(centred * centred, axis=-1, keepdims=True))
    normed = centred * lax.rsqrt(row_var + 1e-06)
    shifted = normed * (1.0 + mod_scale.astype(jnp.float32)[:, None, :]) + mod_shift.astype(jnp.float32)[:, None, :]
    return shifted.astype(jnp.bfloat16)

def head_norm(projected, gain_vector):
    shaped = projected.reshape(projected.shape[:-1] + (-1, gain_vector.shape[0]))
    scaled = shaped * lax.rsqrt(lax.optimization_barrier(jnp.mean(shaped * shaped, axis=-1, keepdims=True)) + 1e-06) * gain_vector
    return scaled.reshape(projected.shape).astype(jnp.bfloat16)

def reference(activations, mod_shift, mod_scale, w_query, w_key, w_value, query_gain, key_gain, stale_keys, stale_values):
    modulated = modulate(activations, mod_shift, mod_scale)
    flat_rows = modulated.reshape(IMAGES * TOKENS, D)
    queries = head_norm(jnp.dot(flat_rows, w_query, preferred_element_type=jnp.float32), query_gain)
    queries = queries.reshape(IMAGES, TOKENS, HEADS, HEAD_DIM)
    fresh_keys = head_norm(jnp.dot(flat_rows, w_key, preferred_element_type=jnp.float32), key_gain)
    fresh_keys = fresh_keys.reshape(IMAGES, TOKENS, HEADS * HEAD_DIM)
    fresh_values = jnp.dot(flat_rows, w_value, preferred_element_type=jnp.float32).astype(jnp.bfloat16)
    fresh_values = fresh_values.reshape(IMAGES, TOKENS, HEADS * HEAD_DIM)
    score_scale = 1.0 / math.sqrt(HEAD_DIM)
    columns = jnp.arange(TOKENS, dtype=jnp.int32) // TOK_DEV
    results = []
    for which_image in range(IMAGES):
        far_keys = stale_keys[which_image].astype(jnp.float32).reshape(TOKENS, HEADS, HEAD_DIM)
        far_values = stale_values[which_image].astype(jnp.float32).reshape(TOKENS, HEADS, HEAD_DIM)
        near_keys = fresh_keys[which_image].astype(jnp.float32).reshape(TOKENS, HEADS, HEAD_DIM)
        near_values = fresh_values[which_image].astype(jnp.float32).reshape(TOKENS, HEADS, HEAD_DIM)
        image_queries = queries[which_image].astype(jnp.float32)

        def attend_patch(patch_id):
            row_start = (patch_id * TOK_DEV).astype(jnp.int32)
            query_block = lax.dynamic_slice_in_dim(image_queries, row_start, TOK_DEV, 0)
            own_keys = lax.dynamic_slice_in_dim(near_keys, row_start, TOK_DEV, 0)
            own_values = lax.dynamic_slice_in_dim(near_values, row_start, TOK_DEV, 0)
            far_scores = jnp.einsum('qhd,khd->hqk', query_block, far_keys) * score_scale
            far_scores = jnp.where((columns == patch_id)[None, None, :], -1e+30, far_scores)
            near_scores = jnp.einsum('qhd,khd->hqk', query_block, own_keys) * score_scale
            row_max = jnp.maximum(lax.optimization_barrier(jnp.max(far_scores, axis=-1)), lax.optimization_barrier(jnp.max(near_scores, axis=-1)))[..., None]
            far_exp = jnp.exp(far_scores - row_max)
            near_exp = jnp.exp(near_scores - row_max)
            weight_total = lax.optimization_barrier(jnp.sum(far_exp, axis=-1)) + lax.optimization_barrier(jnp.sum(near_exp, axis=-1))
            numerator = jnp.einsum('hqk,khd->qhd', far_exp.astype(jnp.bfloat16).astype(jnp.float32), far_values)
            numerator = numerator + jnp.einsum('hqk,khd->qhd', near_exp.astype(jnp.bfloat16).astype(jnp.float32), own_values)
            return (numerator / jnp.transpose(weight_total, (1, 0))[..., None]).astype(jnp.bfloat16)
        patches = jnp.arange(N_PATCH, dtype=jnp.int32)
        blocks = lax.map(attend_patch, patches)
        results.append(blocks.reshape(TOKENS, HEADS * HEAD_DIM))
    attended = jnp.stack(results)
    return (attended, fresh_keys, fresh_values)
```

```python
import math

import jax
import jax.numpy as jnp
from jax import lax
from jax.experimental import pallas as pl
from jax.experimental.pallas import tpu as pltpu
from jax.sharding import Mesh, PartitionSpec as P

HEAD = 128
TOK = 64
IMG = 2
WIDTH = 4096
PART = 1024
COLS = 512
ROWS = IMG * TOK
SCORE = math.log2(math.e) / math.sqrt(HEAD)
F32 = jnp.float32
BF16 = jnp.bfloat16
GROUP = ("zl", "core")


def params(limit):
    return pltpu.CompilerParams(vmem_limit_bytes=limit * 1024 * 1024)


def vmem(count):
    return [pl.BlockSpec(memory_space=pltpu.VMEM)] * count


def smem():
    return pl.BlockSpec(memory_space=pltpu.SMEM)


def dot_t(a, b):
    return lax.dot_general(a, b, (((1,), (1,)), ((), ())), preferred_element_type=F32)


def head_slice(me, d):
    return pl.ds(pl.multiple_of((me ^ d) * HEAD, HEAD), HEAD)


def pack_kernel(me_ref, keys, values, *outs):
    me = me_ref[0]
    for d in range(4):
        cut = head_slice(me, d)
        for i in range(IMG):
            outs[d][i, 0] = keys[i, :, cut]
            outs[d][i, 1] = values[i, :, cut]


def pack(me, keys, values):
    return pl.pallas_call(
        pack_kernel,
        out_shape=[jax.ShapeDtypeStruct((IMG, 2, TOK, HEAD), BF16)] * 4,
        in_specs=[smem()] + vmem(2),
        out_specs=vmem(4),
        compiler_params=params(8),
        name="pack_stale",
    )(me, keys, values)


def project_kernel(idx, x0, x1, x2, x3, m0, m1, m2, m3, wq, wk, wv, qg, kg,
                   q0, q1, q2, q3, qa, fk, fv, xs, acc):
    g = pl.program_id(0)

    @pl.when(g == 0)
    def _():
        blocks = [x[...].astype(F32) for x in (x0, x1, x2, x3)]
        total = sum(jnp.sum(b, axis=-1, keepdims=True) for b in blocks)
        mean = total / WIDTH
        square = sum(jnp.sum((b - mean) * (b - mean), axis=-1, keepdims=True) for b in blocks)
        rstd = lax.rsqrt(square / WIDTH + 1e-06)
        for j, (b, m) in enumerate(zip(blocks, (m0, m1, m2, m3))):
            for i in range(IMG):
                rows = slice(i * TOK, (i + 1) * TOK)
                normed = (b[rows] - mean[rows]) * rstd[rows]
                out = normed * (1.0 + m[IMG + i : IMG + i + 1, :]) + m[i : i + 1, :]
                out = out.astype(BF16)
                xs[2 * j, rows, :] = out[:, : PART // 2]
                xs[2 * j + 1, rows, :] = out[:, PART // 2 :]
        acc[...] = jnp.zeros_like(acc)

    part = xs[g]
    for j, w in enumerate((wq, wk, wv)):
        acc[j] += jnp.dot(part, w[...], preferred_element_type=F32)

    @pl.when(g == pl.num_programs(0) - 1)
    def _():
        for j, (gain, out) in enumerate(((qg, qa), (kg, fk))):
            for h in range(4):
                cut = slice(h * HEAD, (h + 1) * HEAD)
                v = acc[j, :, cut]
                v = v * lax.rsqrt(jnp.mean(v * v, axis=-1, keepdims=True) + 1e-06) * gain[...]
                out[:, cut] = v.astype(BF16)
        fv[...] = acc[2].astype(BF16)
        for d, q in enumerate((q0, q1, q2, q3)):
            q[...] = qa[:, head_slice(idx[4], d)]


def project(idx, xs, ms, weights, gains):
    def whole(shape):
        return pl.BlockSpec(shape, lambda g, idx: (0,) * len(shape))

    def weight_map(g, idx):
        return (idx[g // 2] * 2 + g % 2, 0)

    return pl.pallas_call(
        project_kernel,
        grid_spec=pltpu.PrefetchScalarGridSpec(
            num_scalar_prefetch=1,
            grid=(8,),
            in_specs=[whole((ROWS, PART))] * 4
            + [whole((2 * IMG, PART))] * 4
            + [pl.BlockSpec((PART // 2, COLS), weight_map)] * 3
            + [whole((1, HEAD))] * 2,
            out_specs=[whole((ROWS, HEAD))] * 4 + [whole((ROWS, COLS))] * 3,
            scratch_shapes=[
                pltpu.VMEM((8, ROWS, PART // 2), BF16),
                pltpu.VMEM((3, ROWS, COLS), F32),
            ],
        ),
        out_shape=[jax.ShapeDtypeStruct((ROWS, HEAD), BF16)] * 4
        + [jax.ShapeDtypeStruct((ROWS, COLS), BF16)] * 3,
        compiler_params=params(24),
        name="project",
    )(idx, *xs, *ms, *weights, *gains)


def near_kernel(qa, fk, fv, out, lse):
    lanes = lax.broadcasted_iota(jnp.int32, (TOK, HEAD), 1)
    for i in range(IMG):
        rows = slice(i * TOK, (i + 1) * TOK)
        levels = jnp.zeros((TOK, HEAD), F32)
        for h in range(4):
            cut = slice(h * HEAD, (h + 1) * HEAD)
            s = dot_t(qa[rows, cut], fk[rows, cut]) * SCORE
            top = jnp.max(s, axis=-1, keepdims=True)
            p = jnp.exp2(s - top)
            total = jnp.sum(p, axis=-1, keepdims=True)
            numer = jnp.dot(p.astype(BF16), fv[rows, cut], preferred_element_type=F32)
            out[rows, cut] = numer / total
            levels = jnp.where(lanes == h, top + jnp.log2(total), levels)
        lse[rows, :] = levels


def near(qa, fk, fv):
    return pl.pallas_call(
        near_kernel,
        out_shape=[
            jax.ShapeDtypeStruct((ROWS, COLS), F32),
            jax.ShapeDtypeStruct((ROWS, HEAD), F32),
        ],
        in_specs=vmem(3),
        out_specs=vmem(2),
        compiler_params=params(8),
        name="near",
    )(qa, fk, fv)


def attend_kernel(q0, q1, q2, q3, a0, b0, a1, b1, *outs):
    qs = (q0, q1, q2, q3)
    entries = 16
    count = entries * TOK
    row_patch = lax.broadcasted_iota(jnp.int32, (4 * TOK, 4 * TOK), 0) // TOK
    col_patch = lax.broadcasted_iota(jnp.int32, (4 * TOK, 4 * TOK), 1) // TOK
    own = row_patch == col_patch
    lse_rows = [jnp.zeros((1, HEAD), F32) for _ in range(4)]
    row = lax.broadcasted_iota(jnp.int32, (TOK, HEAD), 0)
    lane = lax.broadcasted_iota(jnp.int32, (TOK, HEAD), 1)
    for i, streams in enumerate(((a0, b0), (a1, b1))):
        q = jnp.concatenate([r[i * TOK : (i + 1) * TOK] for r in qs], axis=0)
        top = total = numer = None
        for stream in streams:
            for c in range(stream.shape[0] // entries):
                span = slice(c * entries, (c + 1) * entries)
                k = stream[span, 0].reshape(count, HEAD)
                v = stream[span, 1].reshape(count, HEAD)
                s = dot_t(q, k) * SCORE
                if top is None:
                    s = jnp.concatenate(
                        [jnp.where(own, -1e30, s[:, : 4 * TOK]), s[:, 4 * TOK :]], axis=1
                    )
                    top = jnp.max(s, axis=-1, keepdims=True)
                    p = jnp.exp2(s - top)
                    total = jnp.sum(p, axis=-1, keepdims=True)
                    numer = jnp.dot(p.astype(BF16), v, preferred_element_type=F32)
                else:
                    new = jnp.maximum(top, jnp.max(s, axis=-1, keepdims=True))
                    factor = jnp.exp2(top - new)
                    p = jnp.exp2(s - new)
                    total = total * factor + jnp.sum(p, axis=-1, keepdims=True)
                    numer = numer * factor + jnp.dot(
                        p.astype(BF16), v, preferred_element_type=F32
                    )
                    top = new
        out = (numer / total).astype(BF16)
        level = top + jnp.log2(total)
        for d in range(4):
            span = slice(d * TOK, (d + 1) * TOK)
            outs[d][i * TOK : (i + 1) * TOK, :] = out[span]
            lse_rows[d] += jnp.sum(
                jnp.where(lane == row + i * TOK, level[span], 0.0), axis=0, keepdims=True
            )
    sub = lax.broadcasted_iota(jnp.int32, (16, HEAD), 0)
    for d in range(4):
        high = lse_rows[d].astype(BF16).astype(F32)
        rest = lse_rows[d] - high
        middle = rest.astype(BF16).astype(F32)
        low = rest - middle
        tail = jnp.where(sub == 0, high, jnp.where(sub == 1, middle, jnp.where(sub == 2, low, 0.0)))
        outs[d][ROWS : ROWS + 16, :] = tail.astype(BF16)


def attend(qs, streams):
    return pl.pallas_call(
        attend_kernel,
        out_shape=[jax.ShapeDtypeStruct((ROWS + 16, HEAD), BF16)] * 4,
        in_specs=vmem(8),
        out_specs=vmem(4),
        compiler_params=params(32),
        name="attend",
    )(*qs, *streams)


def combine_kernel(me_ref, r0, r1, r2, r3, near_out, near_lse, att):
    me = me_ref[0]
    row = lax.broadcasted_iota(jnp.int32, (ROWS, HEAD), 0)
    lane = lax.broadcasted_iota(jnp.int32, (ROWS, HEAD), 1)
    for d, r in enumerate((r0, r1, r2, r3)):
        cut = head_slice(me, d)
        tail = r[ROWS : ROWS + 16, :].astype(F32)
        level = tail[0:1] + tail[1:2] + tail[2:3]
        far_lse = jnp.sum(jnp.where(lane == row, level, 0.0), axis=1, keepdims=True)
        own_lse = jnp.sum(
            jnp.where(lane == (me ^ d), near_lse[...], 0.0), axis=1, keepdims=True
        )
        top = jnp.maximum(far_lse, own_lse)
        far_weight = jnp.exp2(far_lse - top)
        own_weight = jnp.exp2(own_lse - top)
        out = r[:ROWS, :].astype(F32) * far_weight + near_out[:, cut] * own_weight
        att[:, cut] = (out / (far_weight + own_weight)).astype(BF16)


def combine(me, rs, near_out, near_lse):
    return pl.pallas_call(
        combine_kernel,
        out_shape=jax.ShapeDtypeStruct((ROWS, COLS), BF16),
        in_specs=[smem()] + vmem(6),
        out_specs=pl.BlockSpec(memory_space=pltpu.VMEM),
        compiler_params=params(8),
        name="combine",
    )(me, *rs, near_out, near_lse)


def group_swap(parts):
    return [parts[0]] + [
        lax.ppermute(parts[d], GROUP, [(i, i ^ d) for i in range(4)]) for d in (1, 2, 3)
    ]


def swap(value, axis, step):
    flips = ((1, 3), (3, 1))[step]
    if axis == "zh":
        names, far, near_ = ("core", axis), 1, 4
    else:
        names, far, near_ = (axis, "core"), 2, 1
    perm = [
        (a * far + c * near_, (a ^ flips[c]) * far + c * near_)
        for a in range(4)
        for c in range(2)
    ]
    return lax.ppermute(value, names, perm)


def spread(stream, first, second):
    for axis in (first, second):
        for step in range(2):
            other = swap(stream, axis, step)
            if axis == second and step == 1:
                return stream, other
            stream = jnp.concatenate([stream, other], axis=0)


def on_device(activations, mod_shift, mod_scale, w_query, w_key, w_value,
              query_gain, key_gain, stale_keys, stale_values):
    me = lax.axis_index("zl") * 2 + lax.axis_index("core")
    rank = lax.axis_index("zh")
    core = lax.axis_index("core")
    me1 = me.reshape(1).astype(jnp.int32)

    x0 = activations.reshape(ROWS, PART)
    m0 = jnp.concatenate([mod_shift, mod_scale], axis=0).astype(F32)
    x1, x2 = swap(x0, "zh", 0), swap(x0, "zh", 1)
    m1, m2 = swap(m0, "zh", 0), swap(m0, "zh", 1)

    packed = group_swap(pack(me1, stale_keys, stale_values))
    streams = [jnp.stack([p[i] for p in packed], axis=0) for i in range(IMG)]

    x3 = swap(x1, "zh", 1)
    m3 = swap(m1, "zh", 1)
    first = jnp.where(core == 0, 1, 3)
    idx = jnp.stack([rank, rank ^ first, rank ^ (first ^ 2), rank ^ 2, me]).astype(jnp.int32)

    a0, b0 = spread(streams[0], "x", "y")
    a1, b1 = spread(streams[1], "y", "x")

    q0, q1, q2, q3, qa, fk, fv = project(
        idx, (x0, x1, x2, x3), (m0, m1, m2, m3), (w_query, w_key, w_value),
        (query_gain.reshape(1, HEAD), key_gain.reshape(1, HEAD)),
    )
    qs = group_swap([q0, q1, q2, q3])
    near_out, near_lse = near(qa, fk, fv)
    outs = group_swap(attend(qs, (a0, b0, a1, b1)))
    att = combine(me1, outs, near_out, near_lse)
    shape = (IMG, TOK, COLS)
    return att.reshape(shape), fk.reshape(shape), fv.reshape(shape)


def solution(mesh):
    split = Mesh(mesh.devices.reshape(4, 2, 4, 2, 4), ("x", "zl", "y", "core", "zh"))
    patch = ("x", "zl", "y", "core")
    rows = P(None, patch, "zh")
    cols = P(None, "zh")
    return jax.shard_map(
        on_device,
        mesh=split,
        in_specs=(rows, cols, cols, cols, cols, cols, P(), P(), rows, rows),
        out_specs=(rows, rows, rows),
        check_vma=False,
    )
```

```python
import math

import jax
import jax.numpy as jnp
from jax import lax
from jax.experimental import pallas as pl
from jax.experimental.pallas import tpu as pltpu
from jax.sharding import Mesh, PartitionSpec as P

HEAD = 128
TOK = 64
IMG = 2
WIDTH = 4096
PART = 1024
COLS = 512
ROWS = IMG * TOK
SCORE = math.log2(math.e) / math.sqrt(HEAD)
F32 = jnp.float32
BF16 = jnp.bfloat16
GROUP = ("zl", "core")


def params(limit):
    return pltpu.CompilerParams(vmem_limit_bytes=limit * 1024 * 1024)


def vmem(count):
    return [pl.BlockSpec(memory_space=pltpu.VMEM)] * count


def hbm(count):
    return [pl.BlockSpec(memory_space=pltpu.HBM)] * count


def anywhere(count):
    return [pl.BlockSpec(memory_space=pl.ANY)] * count


def smem():
    return pl.BlockSpec(memory_space=pltpu.SMEM)


def dot_t(a, b):
    return lax.dot_general(a, b, (((1,), (1,)), ((), ())), preferred_element_type=F32)


def head_slice(me, d):
    return pl.ds(pl.multiple_of((me ^ d) * HEAD, HEAD), HEAD)


def pack_kernel(me_ref, keys, values, o0, o1, o2, o3, sems):
    copies = []
    for d, out in enumerate((o0, o1, o2, o3)):
        cut = head_slice(me_ref[0], d)
        for i in range(IMG):
            for j, source in enumerate((keys, values)):
                copies.append(
                    pltpu.make_async_copy(
                        source.at[i, :, cut], out.at[i, j], sems.at[len(copies)]
                    )
                )
    for copy in copies:
        copy.start()
    for copy in copies:
        copy.wait()


def pack(me, keys, values):
    return pl.pallas_call(
        pack_kernel,
        out_shape=[jax.ShapeDtypeStruct((IMG, 2, TOK, HEAD), BF16)] * 4,
        in_specs=[smem()] + hbm(2),
        out_specs=vmem(4),
        scratch_shapes=[pltpu.SemaphoreType.DMA((16,))],
        compiler_params=params(56),
        name="pack_stale",
    )(me, keys, values)


def payload_kernel(x, shift, scale, out, sem):
    copy = pltpu.make_async_copy(x, out.at[:ROWS], sem)
    copy.start()
    out[ROWS:] = jnp.zeros((16, PART), BF16)
    out[ROWS : ROWS + IMG] = shift[...]
    out[ROWS + IMG : ROWS + 2 * IMG] = scale[...]
    copy.wait()


def payload(x, shift, scale):
    return pl.pallas_call(
        payload_kernel,
        out_shape=jax.ShapeDtypeStruct((ROWS + 16, PART), BF16),
        in_specs=hbm(1) + vmem(2),
        out_specs=pl.BlockSpec(memory_space=pltpu.VMEM),
        scratch_shapes=[pltpu.SemaphoreType.DMA],
        compiler_params=params(56),
        name="payload",
    )(x, shift, scale)


def tie(values, deps):
    count = len(values)
    return pl.pallas_call(
        lambda *refs: None,
        out_shape=[jax.ShapeDtypeStruct(v.shape, v.dtype) for v in values],
        in_specs=anywhere(count + len(deps)),
        out_specs=anywhere(count),
        input_output_aliases={i: i for i in range(count)},
        compiler_params=params(4),
        name="tie",
    )(*values, *deps)


def join(groups, deps=()):
    counts = [len(g) for g in groups]

    def kernel(*refs):
        ins, outs = refs[: sum(counts)], refs[sum(counts) + len(deps) :]
        at = 0
        for out, count in zip(outs, counts):
            row = 0
            for r in ins[at : at + count]:
                out[row : row + r.shape[0]] = r[...]
                row += r.shape[0]
            at += count

    def shape(group):
        rows = sum(v.shape[0] for v in group)
        return jax.ShapeDtypeStruct((rows,) + group[0].shape[1:], group[0].dtype)

    return pl.pallas_call(
        kernel,
        out_shape=[shape(g) for g in groups],
        in_specs=vmem(sum(counts)) + anywhere(len(deps)),
        out_specs=vmem(len(groups)),
        compiler_params=params(12),
        name="join",
    )(*[v for g in groups for v in g], *deps)


def stack_kernel(p0, p1, p2, p3, s0, s1):
    for d, p in enumerate((p0, p1, p2, p3)):
        s0[d] = p[0]
        s1[d] = p[1]


def stack_images(packed):
    return pl.pallas_call(
        stack_kernel,
        out_shape=[jax.ShapeDtypeStruct((4, 2, TOK, HEAD), BF16)] * IMG,
        in_specs=vmem(4),
        out_specs=vmem(2),
        compiler_params=params(8),
        name="stack_images",
    )(*packed)


def weight_copies(sources, buffers, sems):
    copies = []
    for n, (source, buffer) in enumerate(zip(sources, buffers)):
        for j in range(4):
            rows = pl.ds(j * PART, PART)
            copies.append(
                pltpu.make_async_copy(source.at[rows, :], buffer.at[j], sems.at[4 * n + j])
            )
    for copy in copies:
        copy.start()
    return copies


def project(xs, buffer, copies):
    acc = jnp.zeros((ROWS, COLS), F32)
    for j in range(4):
        copies[j].wait()
        acc += jnp.dot(xs[j], buffer[j], preferred_element_type=F32)
    return acc


def head_norm(v, gain):
    return v * lax.rsqrt(jnp.mean(v * v, axis=-1, keepdims=True) + 1e-06) * gain


def query_kernel(me_ref, x, wq, qg, q0, q1, q2, q3, qa, xs, buffer, sems):
    copies = weight_copies((wq,), (buffer,), sems)
    blocks = [x.at[j] for j in range(4)]
    total = sum(jnp.sum(b[:ROWS].astype(F32), axis=-1, keepdims=True) for b in blocks)
    mean = total / WIDTH
    square = jnp.zeros_like(mean)
    for b in blocks:
        centred = b[:ROWS].astype(F32) - mean
        square += jnp.sum(centred * centred, axis=-1, keepdims=True)
    rstd = lax.rsqrt(square / WIDTH + 1e-06)
    for j, b in enumerate(blocks):
        mods = b[ROWS : ROWS + 16].astype(F32)
        for i in range(IMG):
            rows = slice(i * TOK, (i + 1) * TOK)
            normed = (b[rows].astype(F32) - mean[rows]) * rstd[rows]
            out = normed * (1.0 + mods[IMG + i : IMG + i + 1, :]) + mods[i : i + 1, :]
            xs[j, rows, :] = out.astype(BF16)
    acc = project(xs, buffer, copies)
    for h in range(4):
        cut = slice(h * HEAD, (h + 1) * HEAD)
        qa[:, cut] = head_norm(acc[:, cut], qg[...]).astype(BF16)
    for d, q in enumerate((q0, q1, q2, q3)):
        q[...] = qa[:, head_slice(me_ref[0], d)]


def project_queries(me, x, wq, gain):
    return pl.pallas_call(
        query_kernel,
        out_shape=[jax.ShapeDtypeStruct((ROWS, HEAD), BF16)] * 4
        + [
            jax.ShapeDtypeStruct((ROWS, COLS), BF16),
            jax.ShapeDtypeStruct((4, ROWS, PART), BF16),
        ],
        in_specs=[smem()] + vmem(1) + hbm(1) + vmem(1),
        out_specs=vmem(6),
        scratch_shapes=[pltpu.VMEM((4, PART, COLS), BF16), pltpu.SemaphoreType.DMA((4,))],
        compiler_params=params(50),
        cost_estimate=pl.CostEstimate(
            flops=2 * ROWS * WIDTH * COLS, bytes_accessed=5 << 20, transcendentals=0
        ),
        name="queries",
    )(me, x, wq, gain)


def keys_kernel(xs, wk, kg, fk, buffer, sems):
    acc = project(xs, buffer, weight_copies((wk,), (buffer,), sems))
    for h in range(4):
        cut = slice(h * HEAD, (h + 1) * HEAD)
        fk[:, cut] = head_norm(acc[:, cut], kg[...]).astype(BF16)


def project_keys(xs, wk, gain):
    return pl.pallas_call(
        keys_kernel,
        out_shape=jax.ShapeDtypeStruct((ROWS, COLS), BF16),
        in_specs=vmem(1) + hbm(1) + vmem(1),
        out_specs=pl.BlockSpec(memory_space=pltpu.VMEM),
        scratch_shapes=[pltpu.VMEM((4, PART, COLS), BF16), pltpu.SemaphoreType.DMA((4,))],
        compiler_params=params(50),
        cost_estimate=pl.CostEstimate(
            flops=2 * ROWS * WIDTH * COLS, bytes_accessed=5 << 20, transcendentals=0
        ),
        name="keys",
    )(xs, wk, gain)


def near_kernel(xs, qa, fk, wv, _, fv, out, lse, buffer, sems):
    copies = weight_copies((wv,), (buffer,), sems)
    fv[...] = project(xs, buffer, copies).astype(BF16)
    lanes = lax.broadcasted_iota(jnp.int32, (TOK, HEAD), 1)
    for i in range(IMG):
        rows = slice(i * TOK, (i + 1) * TOK)
        levels = jnp.zeros((TOK, HEAD), F32)
        for h in range(4):
            cut = slice(h * HEAD, (h + 1) * HEAD)
            s = dot_t(qa[rows, cut], fk[rows, cut]) * SCORE
            top = jnp.max(s, axis=-1, keepdims=True)
            p = jnp.exp2(s - top)
            total = jnp.sum(p, axis=-1, keepdims=True)
            numer = jnp.dot(p.astype(BF16), fv[rows, cut], preferred_element_type=F32)
            out[rows, cut] = numer / total
            levels = jnp.where(lanes == h, top + jnp.log2(total), levels)
        lse[rows, :] = levels


def near(xs, qa, fk, wv, dep):
    return pl.pallas_call(
        near_kernel,
        out_shape=[
            jax.ShapeDtypeStruct((ROWS, COLS), BF16),
            jax.ShapeDtypeStruct((ROWS, COLS), F32),
            jax.ShapeDtypeStruct((ROWS, HEAD), F32),
        ],
        in_specs=vmem(3) + hbm(1) + anywhere(1),
        out_specs=vmem(3),
        scratch_shapes=[pltpu.VMEM((4, PART, COLS), BF16), pltpu.SemaphoreType.DMA((4,))],
        compiler_params=params(50),
        cost_estimate=pl.CostEstimate(
            flops=2 * ROWS * WIDTH * COLS, bytes_accessed=6 << 20, transcendentals=0
        ),
        name="near",
    )(xs, qa, fk, wv, dep)


def attend_part(q, stream, state, mask):
    entries = 16
    count = entries * TOK
    for c in range(stream.shape[0] // entries):
        span = slice(c * entries, (c + 1) * entries)
        k = stream[span, 0].reshape(count, HEAD)
        v = stream[span, 1].reshape(count, HEAD)
        s = dot_t(q, k) * SCORE
        if state is None:
            s = jnp.concatenate(
                [jnp.where(mask, -1e30, s[:, : 4 * TOK]), s[:, 4 * TOK :]], axis=1
            )
            top = jnp.max(s, axis=-1, keepdims=True)
            p = jnp.exp2(s - top)
            total = jnp.sum(p, axis=-1, keepdims=True)
            numer = jnp.dot(p.astype(BF16), v, preferred_element_type=F32)
        else:
            old, total, numer = state
            top = jnp.maximum(old, jnp.max(s, axis=-1, keepdims=True))
            factor = jnp.exp2(old - top)
            p = jnp.exp2(s - top)
            total = total * factor + jnp.sum(p, axis=-1, keepdims=True)
            numer = numer * factor + jnp.dot(p.astype(BF16), v, preferred_element_type=F32)
        state = (top, total, numer)
    return state


def image_queries(qs, i):
    return jnp.concatenate([r[i * TOK : (i + 1) * TOK] for r in qs], axis=0)


def attend_first_kernel(q0, q1, q2, q3, s0, u0, s1, u1, _, tops, totals, numers):
    shape = (4 * TOK, 4 * TOK)
    row_patch = lax.broadcasted_iota(jnp.int32, shape, 0) // TOK
    col_patch = lax.broadcasted_iota(jnp.int32, shape, 1) // TOK
    for i, streams in enumerate(((s0, u0), (s1, u1))):
        state = None
        for stream in streams:
            state = attend_part(
                image_queries((q0, q1, q2, q3), i), stream, state, row_patch == col_patch
            )
        top, total, numer = state
        tops[i] = jnp.broadcast_to(top, (4 * TOK, HEAD))
        totals[i] = jnp.broadcast_to(total, (4 * TOK, HEAD))
        numers[i] = numer


def attend_first(qs, streams, dep):
    return pl.pallas_call(
        attend_first_kernel,
        out_shape=[jax.ShapeDtypeStruct((IMG, 4 * TOK, HEAD), F32)] * 3,
        in_specs=vmem(8) + anywhere(1),
        out_specs=vmem(3),
        compiler_params=params(24),
        name="attend_first",
    )(*qs, *streams, dep)


def attend_last_kernel(q0, q1, q2, q3, s0, u0, s1, u1, tops, totals, numers, *outs):
    lse_rows = [jnp.zeros((1, HEAD), F32) for _ in range(4)]
    row = lax.broadcasted_iota(jnp.int32, (TOK, HEAD), 0)
    lane = lax.broadcasted_iota(jnp.int32, (TOK, HEAD), 1)
    for i, streams in enumerate(((s0, u0), (s1, u1))):
        state = (tops[i, :, :1], totals[i, :, :1], numers[i])
        for stream in streams:
            state = attend_part(image_queries((q0, q1, q2, q3), i), stream, state, None)
        top, total, numer = state
        out = (numer / total).astype(BF16)
        level = top + jnp.log2(total)
        for d in range(4):
            span = slice(d * TOK, (d + 1) * TOK)
            outs[d][i * TOK : (i + 1) * TOK, :] = out[span]
            lse_rows[d] += jnp.sum(
                jnp.where(lane == row + i * TOK, level[span], 0.0), axis=0, keepdims=True
            )
    sub = lax.broadcasted_iota(jnp.int32, (16, HEAD), 0)
    for d in range(4):
        high = lse_rows[d].astype(BF16).astype(F32)
        rest = lse_rows[d] - high
        middle = rest.astype(BF16).astype(F32)
        low = rest - middle
        tail = jnp.where(sub == 0, high, jnp.where(sub == 1, middle, jnp.where(sub == 2, low, 0.0)))
        outs[d][ROWS : ROWS + 16, :] = tail.astype(BF16)


def attend_last(qs, streams, state):
    return pl.pallas_call(
        attend_last_kernel,
        out_shape=[jax.ShapeDtypeStruct((ROWS + 16, HEAD), BF16)] * 4,
        in_specs=vmem(11),
        out_specs=vmem(4),
        compiler_params=params(24),
        name="attend_last",
    )(*qs, *streams, *state)


def combine_kernel(me_ref, r0, r1, r2, r3, near_out, near_lse, att):
    me = me_ref[0]
    row = lax.broadcasted_iota(jnp.int32, (ROWS, HEAD), 0)
    lane = lax.broadcasted_iota(jnp.int32, (ROWS, HEAD), 1)
    for d, r in enumerate((r0, r1, r2, r3)):
        cut = head_slice(me, d)
        tail = r[ROWS : ROWS + 16, :].astype(F32)
        level = tail[0:1] + tail[1:2] + tail[2:3]
        far_lse = jnp.sum(jnp.where(lane == row, level, 0.0), axis=1, keepdims=True)
        own_lse = jnp.sum(
            jnp.where(lane == (me ^ d), near_lse[...], 0.0), axis=1, keepdims=True
        )
        top = jnp.maximum(far_lse, own_lse)
        far_weight = jnp.exp2(far_lse - top)
        own_weight = jnp.exp2(own_lse - top)
        out = r[:ROWS, :].astype(F32) * far_weight + near_out[:, cut] * own_weight
        att[:, cut] = (out / (far_weight + own_weight)).astype(BF16)


def combine(me, rs, near_out, near_lse):
    return pl.pallas_call(
        combine_kernel,
        out_shape=jax.ShapeDtypeStruct((ROWS, COLS), BF16),
        in_specs=[smem()] + vmem(6),
        out_specs=pl.BlockSpec(memory_space=pltpu.VMEM),
        compiler_params=params(8),
        name="combine",
    )(me, *rs, near_out, near_lse)


def group_swap(parts):
    return [parts[0]] + [
        lax.ppermute(parts[d], GROUP, [(i, i ^ d) for i in range(4)]) for d in (1, 2, 3)
    ]


def swap(value, axis, step):
    flips = ((1, 3), (3, 1))[step]
    if axis == "zh":
        names, far, near_ = ("core", axis), 1, 4
    else:
        names, far, near_ = (axis, "core"), 2, 1
    perm = [
        (a * far + c * near_, (a ^ flips[c]) * far + c * near_)
        for a in range(4)
        for c in range(2)
    ]
    return lax.ppermute(value, names, perm)


def on_device(activations, mod_shift, mod_scale, w_query, w_key, w_value,
              query_gain, key_gain, stale_keys, stale_values):
    me = lax.axis_index("zl") * 2 + lax.axis_index("core")
    me1 = me.reshape(1).astype(jnp.int32)

    x0 = payload(activations.reshape(ROWS, PART), mod_shift, mod_scale)
    xall = lax.all_gather(x0, "zh")

    parts = group_swap(pack(me1, stale_keys, stale_values))
    s0, s1 = stack_images(parts)
    s0, s1 = join([(s0, swap(s0, "x", 0)), (s1, swap(s1, "y", 0))])
    s0, s1 = join([(s0, swap(s0, "x", 1)), (s1, swap(s1, "y", 1))])

    u0, u1 = swap(s0, "y", 0), swap(s1, "x", 0)
    v0, v1 = swap(s0, "y", 1), swap(s1, "x", 1)
    w0, w1 = swap(u0, "y", 1), swap(u1, "x", 1)

    q0, q1, q2, q3, qa, xs = project_queries(me1, xall, w_query, query_gain.reshape(1, HEAD))
    qs = group_swap([q0, q1, q2, q3])
    fk = project_keys(xs, w_key, key_gain.reshape(1, HEAD))
    state = attend_first(qs, (s0, u0, s1, u1), fk)
    outs = attend_last(qs, (v0, w0, v1, w1), state)
    fv, near_out, near_lse = near(xs, qa, fk, w_value, outs[0])
    outs = group_swap(outs)
    att = combine(me1, outs, near_out, near_lse)
    shape = (IMG, TOK, COLS)
    return att.reshape(shape), fk.reshape(shape), fv.reshape(shape)


def solution(mesh):
    split = Mesh(mesh.devices.reshape(4, 2, 4, 2, 4), ("x", "zl", "y", "core", "zh"))
    patch = ("x", "zl", "y", "core")
    rows = P(None, patch, "zh")
    cols = P(None, "zh")
    return jax.shard_map(
        on_device,
        mesh=split,
        in_specs=(rows, cols, cols, cols, cols, cols, P(), P(), rows, rows),
        out_specs=(rows, rows, rows),
        check_vma=False,
    )
```

```python
import math

import jax
import jax.numpy as jnp
from jax import lax
from jax.experimental import pallas as pl
from jax.experimental.pallas import tpu as pltpu
from jax.sharding import Mesh, PartitionSpec as P

HEAD = 128
TOK = 64
IMG = 2
WIDTH = 4096
PART = 1024
COLS = 512
ROWS = IMG * TOK
SCORE = math.log2(math.e) / math.sqrt(HEAD)
F32 = jnp.float32
BF16 = jnp.bfloat16
FLIP = [(0, 1), (1, 0)]


def params(limit):
    return pltpu.CompilerParams(vmem_limit_bytes=limit * 1024 * 1024)


def vmem(count):
    return [pl.BlockSpec(memory_space=pltpu.VMEM)] * count


def hbm(count):
    return [pl.BlockSpec(memory_space=pltpu.HBM)] * count


def anywhere(count):
    return [pl.BlockSpec(memory_space=pl.ANY)] * count


def smem():
    return pl.BlockSpec(memory_space=pltpu.SMEM)


def dot_t(a, b):
    return lax.dot_general(a, b, (((1,), (1,)), ((), ())), preferred_element_type=F32)


def head_of(code, d):
    core, y = code[0] & 1, (code[0] >> 1) & 3
    side = core ^ (d >> 1)
    bit = jnp.where(side == 0, (y ^ (y >> 1)) & 1, y >> 1)
    return 2 * side + (bit ^ (d & 1))


def head_slice(code, d):
    return pl.ds(pl.multiple_of(head_of(code, d) * HEAD, HEAD), HEAD)


def rank_of(code, j):
    flips = (0, jnp.where(code[0] & 1 == 0, 1, 3), jnp.where(code[0] & 1 == 0, 3, 1), 2)
    return (code[0] >> 3) ^ flips[j]


def pack_kernel(heads, keys, values, x, shift, scale, own, next_, other, pay, sems):
    copies = []

    def copy(source, target):
        copies.append(pltpu.make_async_copy(source, target, sems.at[len(copies)]))
        copies[-1].start()

    copy(x, pay.at[:ROWS])
    for d, out in ((2, other.at[0]), (3, other.at[1]), (1, next_), (0, own)):
        cut = head_slice(heads, d)
        for i in range(IMG):
            for j, source in enumerate((keys, values)):
                copy(source.at[i, :, cut], out.at[i, j])
    pay[ROWS:] = jnp.zeros((16, PART), BF16)
    pay[ROWS : ROWS + IMG] = shift[...]
    pay[ROWS + IMG : ROWS + 2 * IMG] = scale[...]
    for one in copies:
        one.wait()


def pack(heads, keys, values, x, shift, scale):
    shape = (IMG, 2, TOK, HEAD)
    return pl.pallas_call(
        pack_kernel,
        out_shape=[
            jax.ShapeDtypeStruct(shape, BF16),
            jax.ShapeDtypeStruct(shape, BF16),
            jax.ShapeDtypeStruct((2,) + shape, BF16),
            jax.ShapeDtypeStruct((ROWS + 16, PART), BF16),
        ],
        in_specs=[smem()] + hbm(3) + vmem(2),
        out_specs=vmem(4),
        scratch_shapes=[pltpu.SemaphoreType.DMA((17,))],
        compiler_params=params(56),
        name="pack",
    )(heads, keys, values, x, shift, scale)


def call(kernel, name, limit, shapes, operands, deps=()):
    return pl.pallas_call(
        kernel,
        out_shape=[jax.ShapeDtypeStruct(s, BF16) for s in shapes],
        in_specs=vmem(len(operands)) + anywhere(len(deps)),
        out_specs=vmem(len(shapes)),
        compiler_params=params(limit),
        name=name,
    )(*operands, *deps)


def join(groups, deps=()):
    counts = [len(g) for g in groups]

    def kernel(*refs):
        ins, outs = refs[: sum(counts)], refs[sum(counts) + len(deps) :]
        at = 0
        for out, count in zip(outs, counts):
            row = 0
            for r in ins[at : at + count]:
                out[row : row + r.shape[0]] = r[...]
                row += r.shape[0]
            at += count

    def shape(group):
        rows = sum(v.shape[0] for v in group)
        return jax.ShapeDtypeStruct((rows,) + group[0].shape[1:], group[0].dtype)

    return pl.pallas_call(
        kernel,
        out_shape=[shape(g) for g in groups],
        in_specs=vmem(sum(counts)) + anywhere(len(deps)),
        out_specs=vmem(len(groups)),
        compiler_params=params(12),
        name="join",
    )(*[v for g in groups for v in g], *deps)


def pair_kernel(a, b, out):
    out[0] = a[...]
    out[1] = b[1]


def stack_kernel(own, other, far, s0, s1):
    for i, s in enumerate((s0, s1)):
        s[0] = own[i]
        s[1] = other[0, i]
        s[2] = far[0, i]
        s[3] = far[1, i]


def query_pairs_kernel(own, next_, other, g, n):
    g[0] = own[...]
    g[1] = other[0]
    n[0] = next_[...]
    n[1] = other[1]


def back_kernel(g, y, z, d, _, out):
    for j, r in enumerate((g, z, y, d)):
        out[j] = r[1]


def weight_copies(idx, sources, buffers, sems):
    copies = []
    for n, (source, buffer) in enumerate(zip(sources, buffers)):
        for j in range(4):
            rows = pl.ds(pl.multiple_of(rank_of(idx, j) * PART, PART), PART)
            copies.append(
                pltpu.make_async_copy(source.at[rows, :], buffer.at[j], sems.at[4 * n + j])
            )
    for copy in copies:
        copy.start()
    return copies


def project(xs, buffer, copies):
    acc = jnp.zeros((ROWS, COLS), F32)
    for j in range(4):
        copies[j].wait()
        acc += jnp.dot(xs[j], buffer[j], preferred_element_type=F32)
    return acc


def head_norm(v, gain):
    return v * lax.rsqrt(jnp.mean(v * v, axis=-1, keepdims=True) + 1e-06) * gain


def query_kernel(idx, x0, x1, x2, x3, wq, qg, own, next_, other, qa, xs, buffer, sems):
    copies = weight_copies(idx, (wq,), (buffer,), sems)
    blocks = (x0, x1, x2, x3)
    total = sum(jnp.sum(b[:ROWS].astype(F32), axis=-1, keepdims=True) for b in blocks)
    mean = total / WIDTH
    square = jnp.zeros_like(mean)
    for b in blocks:
        centred = b[:ROWS].astype(F32) - mean
        square += jnp.sum(centred * centred, axis=-1, keepdims=True)
    rstd = lax.rsqrt(square / WIDTH + 1e-06)
    for j, b in enumerate(blocks):
        mods = b[ROWS : ROWS + 16].astype(F32)
        for i in range(IMG):
            rows = slice(i * TOK, (i + 1) * TOK)
            normed = (b[rows].astype(F32) - mean[rows]) * rstd[rows]
            out = normed * (1.0 + mods[IMG + i : IMG + i + 1, :]) + mods[i : i + 1, :]
            xs[j, rows, :] = out.astype(BF16)
    acc = project(xs, buffer, copies)
    for h in range(4):
        cut = slice(h * HEAD, (h + 1) * HEAD)
        qa[:, cut] = head_norm(acc[:, cut], qg[:1]).astype(BF16)
    own[...] = qa[:, head_slice(idx, 0)]
    next_[...] = qa[:, head_slice(idx, 1)]
    for j in range(2):
        other[j] = qa[:, head_slice(idx, 2 + j)]


def project_queries(idx, xs, wq, gain):
    return pl.pallas_call(
        query_kernel,
        out_shape=[
            jax.ShapeDtypeStruct((ROWS, HEAD), BF16),
            jax.ShapeDtypeStruct((ROWS, HEAD), BF16),
            jax.ShapeDtypeStruct((2, ROWS, HEAD), BF16),
            jax.ShapeDtypeStruct((ROWS, COLS), BF16),
            jax.ShapeDtypeStruct((4, ROWS, PART), BF16),
        ],
        in_specs=[smem()] + vmem(4) + hbm(1) + vmem(1),
        out_specs=vmem(5),
        scratch_shapes=[pltpu.VMEM((4, PART, COLS), BF16), pltpu.SemaphoreType.DMA((4,))],
        compiler_params=params(50),
        cost_estimate=pl.CostEstimate(
            flops=2 * ROWS * WIDTH * COLS, bytes_accessed=5 << 20, transcendentals=0
        ),
        name="queries",
    )(idx, *xs, wq, gain)


def fresh_kernel(idx, xs, qa, wk, wv, kg, _, fk, fv, out, lse, kbuf, vbuf, sems):
    copies = weight_copies(idx, (wk, wv), (kbuf, vbuf), sems)
    acc = project(xs, kbuf, copies[:4])
    for h in range(4):
        cut = slice(h * HEAD, (h + 1) * HEAD)
        fk[:, cut] = head_norm(acc[:, cut], kg[1:]).astype(BF16)
    fv[...] = project(xs, vbuf, copies[4:]).astype(BF16)
    lanes = lax.broadcasted_iota(jnp.int32, (TOK, HEAD), 1)
    for i in range(IMG):
        rows = slice(i * TOK, (i + 1) * TOK)
        levels = jnp.zeros((TOK, HEAD), F32)
        for h in range(4):
            cut = slice(h * HEAD, (h + 1) * HEAD)
            s = dot_t(qa[rows, cut], fk[rows, cut]) * SCORE
            top = jnp.max(s, axis=-1, keepdims=True)
            p = jnp.exp2(s - top)
            total = jnp.sum(p, axis=-1, keepdims=True)
            numer = jnp.dot(p.astype(BF16), fv[rows, cut], preferred_element_type=F32)
            out[rows, cut] = numer / total
            levels = jnp.where(lanes == h, top + jnp.log2(total), levels)
        lse[rows, :] = levels


def fresh(idx, xs, qa, wk, wv, gain, dep):
    return pl.pallas_call(
        fresh_kernel,
        out_shape=[jax.ShapeDtypeStruct((ROWS, COLS), BF16)] * 2
        + [
            jax.ShapeDtypeStruct((ROWS, COLS), F32),
            jax.ShapeDtypeStruct((ROWS, HEAD), F32),
        ],
        in_specs=[smem()] + vmem(2) + hbm(2) + vmem(1) + anywhere(1),
        out_specs=vmem(4),
        scratch_shapes=[pltpu.VMEM((4, PART, COLS), BF16)] * 2
        + [pltpu.SemaphoreType.DMA((8,))],
        compiler_params=params(50),
        cost_estimate=pl.CostEstimate(
            flops=4 * ROWS * WIDTH * COLS, bytes_accessed=9 << 20, transcendentals=0
        ),
        name="fresh",
    )(idx, xs, qa, wk, wv, gain, dep)


def attend_part(q, stream, state, mask):
    entries = 16
    count = entries * TOK
    for c in range(stream.shape[0] // entries):
        span = slice(c * entries, (c + 1) * entries)
        k = stream[span, 0].reshape(count, HEAD)
        v = stream[span, 1].reshape(count, HEAD)
        s = dot_t(q, k) * SCORE
        if state is None:
            s = jnp.concatenate(
                [jnp.where(mask, -1e30, s[:, : 4 * TOK]), s[:, 4 * TOK :]], axis=1
            )
            top = jnp.max(s, axis=-1, keepdims=True)
            p = jnp.exp2(s - top)
            total = jnp.sum(p, axis=-1, keepdims=True)
            numer = jnp.dot(p.astype(BF16), v, preferred_element_type=F32)
        else:
            old, total, numer = state
            top = jnp.maximum(old, jnp.max(s, axis=-1, keepdims=True))
            factor = jnp.exp2(old - top)
            p = jnp.exp2(s - top)
            total = total * factor + jnp.sum(p, axis=-1, keepdims=True)
            numer = numer * factor + jnp.dot(p.astype(BF16), v, preferred_element_type=F32)
        state = (top, total, numer)
    return state


def attend_kernel(g, n, gz, nd, s0, t0, s1, t1, *outs):
    groups = (g, n, gz, nd)
    count = 2 * len(groups)
    shape = (count * TOK, 4 * TOK)
    row_patch = lax.broadcasted_iota(jnp.int32, shape, 0) // TOK
    col_patch = lax.broadcasted_iota(jnp.int32, shape, 1) // TOK
    lse_rows = [jnp.zeros((1, HEAD), F32) for _ in range(count)]
    row = lax.broadcasted_iota(jnp.int32, (TOK, HEAD), 0)
    lane = lax.broadcasted_iota(jnp.int32, (TOK, HEAD), 1)
    for i, streams in enumerate(((s0, t0), (s1, t1))):
        q = jnp.concatenate(
            [r[j, i * TOK : (i + 1) * TOK] for r in groups for j in range(2)], axis=0
        )
        state = None
        for stream in streams:
            state = attend_part(q, stream, state, row_patch == col_patch)
        top, total, numer = state
        out = (numer / total).astype(BF16)
        level = top + jnp.log2(total)
        for d in range(count):
            span = slice(d * TOK, (d + 1) * TOK)
            outs[d // 2][d % 2, i * TOK : (i + 1) * TOK, :] = out[span]
            lse_rows[d] += jnp.sum(
                jnp.where(lane == row + i * TOK, level[span], 0.0), axis=0, keepdims=True
            )
    sub = lax.broadcasted_iota(jnp.int32, (16, HEAD), 0)
    for d in range(count):
        high = lse_rows[d].astype(BF16).astype(F32)
        rest = lse_rows[d] - high
        middle = rest.astype(BF16).astype(F32)
        low = rest - middle
        tail = jnp.where(sub == 0, high, jnp.where(sub == 1, middle, jnp.where(sub == 2, low, 0.0)))
        outs[d // 2][d % 2, ROWS : ROWS + 16, :] = tail.astype(BF16)


def attend(groups, streams):
    return pl.pallas_call(
        attend_kernel,
        out_shape=[jax.ShapeDtypeStruct((2, ROWS + 16, HEAD), BF16)] * 4,
        in_specs=vmem(8),
        out_specs=vmem(4),
        compiler_params=params(32),
        name="attend",
    )(*groups, *streams)


def combine_kernel(heads, g, z, y, d, other, near_out, near_lse, att):
    row = lax.broadcasted_iota(jnp.int32, (ROWS, HEAD), 0)
    lane = lax.broadcasted_iota(jnp.int32, (ROWS, HEAD), 1)
    halves = ((g.at[0], z.at[0]), (y.at[0], d.at[0]), (other.at[0], other.at[1]),
              (other.at[2], other.at[3]))
    for h, pair in enumerate(halves):
        cut = head_slice(heads, h)
        levels = [
            jnp.sum(jnp.where(lane == head_of(heads, h), near_lse[...], 0.0), axis=1, keepdims=True)
        ]
        parts = [near_out[:, cut]]
        for r in pair:
            tail = r[ROWS : ROWS + 16, :].astype(F32)
            level = tail[0:1] + tail[1:2] + tail[2:3]
            levels.append(jnp.sum(jnp.where(lane == row, level, 0.0), axis=1, keepdims=True))
            parts.append(r[:ROWS, :].astype(F32))
        top = jnp.maximum(jnp.maximum(levels[0], levels[1]), levels[2])
        weights = [jnp.exp2(level - top) for level in levels]
        out = sum(w * p for w, p in zip(weights, parts))
        att[:, cut] = (out / sum(weights)).astype(BF16)


def combine(heads, parts, near_out, near_lse):
    return pl.pallas_call(
        combine_kernel,
        out_shape=jax.ShapeDtypeStruct((ROWS, COLS), BF16),
        in_specs=[smem()] + vmem(7),
        out_specs=pl.BlockSpec(memory_space=pltpu.VMEM),
        compiler_params=params(8),
        name="combine",
    )(heads, *parts, near_out, near_lse)


def swap(value, axis, step):
    flips = ((1, 3), (3, 1))[step]
    if axis == "zh":
        names, far, near_ = ("core", axis), 1, 4
    else:
        names, far, near_ = (axis, "core"), 2, 1
    perm = [
        (a * far + c * near_, (a ^ flips[c]) * far + c * near_)
        for a in range(4)
        for c in range(2)
    ]
    return lax.ppermute(value, names, perm)


def diagonal(value):
    perm = [
        (z * 8 + y * 2 + c, (z ^ 1) * 8 + (y ^ (1, 3)[c]) * 2 + c)
        for z in range(2)
        for y in range(4)
        for c in range(2)
    ]
    return lax.ppermute(value, ("zl", "y", "core"), perm)


def on_device(activations, mod_shift, mod_scale, w_query, w_key, w_value,
              query_gain, key_gain, stale_keys, stale_values):
    code = lax.axis_index("zh") * 8 + lax.axis_index("y") * 2 + lax.axis_index("core")
    code = code.astype(jnp.int32).reshape(1)

    own, next_, other, x0 = pack(
        code, stale_keys, stale_values, activations.reshape(ROWS, PART), mod_shift, mod_scale
    )
    x1, x2 = swap(x0, "zh", 0), swap(x0, "zh", 1)
    other = lax.ppermute(other, "core", FLIP)
    shape = (IMG, 2, TOK, HEAD)
    (far,) = call(pair_kernel, "pair", 8, [(2,) + shape], (next_, other))
    far = swap(far, "y", 0)
    s0, s1 = call(stack_kernel, "stack", 8, [(4,) + shape[1:]] * 2, (own, other, far))
    gains = (query_gain.reshape(1, HEAD), key_gain.reshape(1, HEAD))
    s0, s1, x0, gains = join(
        [(s0, swap(s0, "y", 1)), (s1, swap(s1, "x", 0)), (x0,), gains], (x1, x2)
    )
    x3 = swap(x1, "zh", 1)
    own, next_, other, qa, xs = project_queries(
        code, (x0, x1, x2, x3), w_query, gains
    )
    s0, s1 = join([(s0, swap(s0, "x", 0)), (s1, swap(s1, "x", 1))], (own,))
    t0, t1 = swap(s0, "x", 1), swap(s1, "y", 1)

    other = lax.ppermute(other, "core", FLIP)
    g, n = call(query_pairs_kernel, "query_pairs", 8, [(2, ROWS, HEAD)] * 2, (own, next_, other))
    groups = (g, swap(n, "y", 0), lax.ppermute(g, "zl", FLIP), diagonal(n))
    pg, py, pz, pd = attend(groups, (s0, t0, s1, t1))
    fk, fv, near_out, near_lse = fresh(
        code, xs, qa, w_key, w_value, gains, py
    )
    py, pz, pd = swap(py, "y", 0), lax.ppermute(pz, "zl", FLIP), diagonal(pd)
    (back,) = call(
        back_kernel, "back", 8, [(4, ROWS + 16, HEAD)], (pg, py, pz, pd), (near_lse,)
    )
    back = lax.ppermute(back, "core", FLIP)
    att = combine(code, (pg, pz, py, pd, back), near_out, near_lse)
    shape = (IMG, TOK, COLS)
    return att.reshape(shape), fk.reshape(shape), fv.reshape(shape)


def solution(mesh):
    split = Mesh(mesh.devices.reshape(4, 2, 4, 2, 4), ("x", "zl", "y", "core", "zh"))
    patch = ("x", "zl", "y", "core")
    rows = P(None, patch, "zh")
    cols = P(None, "zh")
    return jax.shard_map(
        on_device,
        mesh=split,
        in_specs=(rows, cols, cols, cols, cols, cols, P(), P(), rows, rows),
        out_specs=(rows, rows, rows),
        check_vma=False,
    )
```

```python
import functools
import math

import jax
import jax.numpy as jnp
from jax import lax
from jax.experimental import pallas as pl
from jax.experimental.pallas import tpu as pltpu
from jax.sharding import Mesh, PartitionSpec as P

HEAD = 128
TOK = 64
IMG = 2
WIDTH = 4096
PART = 1024
COLS = 512
ROWS = IMG * TOK
SCORE = math.log2(math.e) / math.sqrt(HEAD)
F32 = jnp.float32
BF16 = jnp.bfloat16
FLIP = [(0, 1), (1, 0)]


def params(limit):
    return pltpu.CompilerParams(vmem_limit_bytes=limit * 1024 * 1024)


def vmem(count):
    return [pl.BlockSpec(memory_space=pltpu.VMEM)] * count


def hbm(count):
    return [pl.BlockSpec(memory_space=pltpu.HBM)] * count


def anywhere(count):
    return [pl.BlockSpec(memory_space=pl.ANY)] * count


def smem():
    return pl.BlockSpec(memory_space=pltpu.SMEM)


def dot_t(a, b):
    return lax.dot_general(a, b, (((1,), (1,)), ((), ())), preferred_element_type=F32)


def head_of(code, d):
    core, y = code[0] & 1, (code[0] >> 1) & 3
    side = core ^ (d >> 1)
    bit = jnp.where(side == 0, (y ^ (y >> 1)) & 1, y >> 1)
    return 2 * side + (bit ^ (d & 1))


def head_slice(code, d):
    return pl.ds(pl.multiple_of(head_of(code, d) * HEAD, HEAD), HEAD)


def rank_of(code, j):
    flips = (0, jnp.where(code[0] & 1 == 0, 1, 3), jnp.where(code[0] & 1 == 0, 3, 1), 2)
    return (code[0] >> 3) ^ flips[j]


def pack_kernel(heads, keys, values, x, shift, scale, own, next_, other, pay, mods, sems):
    copies = []

    def copy(source, target):
        copies.append(pltpu.make_async_copy(source, target, sems.at[len(copies)]))
        copies[-1].start()

    copy(shift, mods.at[0])
    copy(scale, mods.at[1])
    copy(x, pay.at[:ROWS])
    for d, out in ((2, other.at[0]), (3, other.at[1]), (1, next_), (0, own)):
        cut = head_slice(heads, d)
        for i in range(IMG):
            for j, source in enumerate((keys, values)):
                copy(source.at[i, :, cut], out.at[i, j])
    for one in copies[:2]:
        one.wait()
    pay[ROWS:] = jnp.zeros((16, PART), BF16)
    pay[ROWS : ROWS + IMG] = mods[0]
    pay[ROWS + IMG : ROWS + 2 * IMG] = mods[1]
    for one in copies[2:]:
        one.wait()


def pack(heads, keys, values, x, shift, scale):
    shape = (IMG, 2, TOK, HEAD)
    return pl.pallas_call(
        pack_kernel,
        out_shape=[
            jax.ShapeDtypeStruct(shape, BF16),
            jax.ShapeDtypeStruct(shape, BF16),
            jax.ShapeDtypeStruct((2,) + shape, BF16),
            jax.ShapeDtypeStruct((ROWS + 16, PART), BF16),
        ],
        in_specs=[smem()] + hbm(5),
        out_specs=vmem(4),
        scratch_shapes=[pltpu.VMEM((2, IMG, PART), BF16), pltpu.SemaphoreType.DMA((19,))],
        compiler_params=params(56),
        name="pack",
    )(heads, keys, values, x, shift, scale)


def call(kernel, name, limit, shapes, operands, deps=()):
    return pl.pallas_call(
        kernel,
        out_shape=[jax.ShapeDtypeStruct(s, BF16) for s in shapes],
        in_specs=vmem(len(operands)) + anywhere(len(deps)),
        out_specs=vmem(len(shapes)),
        compiler_params=params(limit),
        name=name,
    )(*operands, *deps)


def join(groups, deps=()):
    counts = [len(g) for g in groups]

    def kernel(*refs):
        ins, outs = refs[: sum(counts)], refs[sum(counts) + len(deps) :]
        at = 0
        for out, count in zip(outs, counts):
            row = 0
            for r in ins[at : at + count]:
                out[row : row + r.shape[0]] = r[...]
                row += r.shape[0]
            at += count

    def shape(group):
        rows = sum(v.shape[0] for v in group)
        return jax.ShapeDtypeStruct((rows,) + group[0].shape[1:], group[0].dtype)

    return pl.pallas_call(
        kernel,
        out_shape=[shape(g) for g in groups],
        in_specs=vmem(sum(counts)) + anywhere(len(deps)),
        out_specs=vmem(len(groups)),
        compiler_params=params(12),
        name="join",
    )(*[v for g in groups for v in g], *deps)


def hold(x0, own, gains):
    def kernel(x_in, own_in, qg, kg, x_out, own_out, gains_out):
        x_out[...] = x_in[...]
        own_out[...] = own_in[...]
        gains_out[:1] = qg[...]
        gains_out[1:] = kg[...]

    return pl.pallas_call(
        kernel,
        out_shape=[
            jax.ShapeDtypeStruct(x0.shape, BF16),
            jax.ShapeDtypeStruct(own.shape, BF16),
            jax.ShapeDtypeStruct((2, HEAD), F32),
        ],
        in_specs=vmem(4),
        out_specs=vmem(3),
        compiler_params=params(8),
        cost_estimate=pl.CostEstimate(flops=0, bytes_accessed=32 << 20, transcendentals=0),
        name="hold",
    )(x0, own, *gains)


def mods_kernel(x, out):
    out[...] = x[ROWS:]


def pair_kernel(a, b, out):
    out[0] = a[...]
    out[1] = b[1]


def stack_kernel(own, other, far, _, s0, s1):
    for i, s in enumerate((s0, s1)):
        s[0] = own[i]
        s[1] = other[0, i]
        s[2] = far[0, i]
        s[3] = far[1, i]


def query_pairs_kernel(own, next_, other, g, n):
    g[0] = own[...]
    g[1] = other[0]
    n[0] = next_[...]
    n[1] = other[1]


def back_kernel(g, y, z, d, _, out):
    for j, r in enumerate((g, z, y, d)):
        out[j] = r[1]


def weight_copies(idx, sources, buffers, sems):
    copies = []
    for n, (source, buffer) in enumerate(zip(sources, buffers)):
        for j in range(4):
            rows = pl.ds(pl.multiple_of(rank_of(idx, j) * PART, PART), PART)
            copies.append(
                pltpu.make_async_copy(source.at[rows, :], buffer.at[j], sems.at[4 * n + j])
            )
    for copy in copies:
        copy.start()
    return copies


def project_copied(xs, buffer, copies):
    acc = jnp.zeros((ROWS, COLS), F32)
    for j in range(4):
        copies[j].wait()
        acc += jnp.dot(xs[j], buffer[j], preferred_element_type=F32)
    return acc


def project(code, xs, w):
    acc = jnp.zeros((ROWS, COLS), F32)
    for j in range(4):
        rows = pl.ds(pl.multiple_of(rank_of(code, j) * PART, PART), PART)
        acc += jnp.dot(xs[j], w[rows, :], preferred_element_type=F32)
    return acc


def head_norm(v, gain):
    return v * lax.rsqrt(jnp.mean(v * v, axis=-1, keepdims=True) + 1e-06) * gain


def query_kernel(idx, x0, x1, x2, x3, m2, wq, qg, own, next_, other, qa, xs, buffer, sems):
    copies = weight_copies(idx, (wq,), (buffer,), sems)
    blocks = (x0, x1, x2, x3)
    total = sum(jnp.sum(b[:ROWS].astype(F32), axis=-1, keepdims=True) for b in blocks)
    mean = total / WIDTH
    square = jnp.zeros_like(mean)
    for b in blocks:
        centred = b[:ROWS].astype(F32) - mean
        square += jnp.sum(centred * centred, axis=-1, keepdims=True)
    rstd = lax.rsqrt(square / WIDTH + 1e-06)
    for j, b in enumerate(blocks):
        mods = (m2[...] if j == 2 else b[ROWS : ROWS + 16]).astype(F32)
        for i in range(IMG):
            rows = slice(i * TOK, (i + 1) * TOK)
            normed = (b[rows].astype(F32) - mean[rows]) * rstd[rows]
            out = normed * (1.0 + mods[IMG + i : IMG + i + 1, :]) + mods[i : i + 1, :]
            xs[j, rows, :] = out.astype(BF16)
    acc = project_copied(xs, buffer, copies)
    for h in range(4):
        cut = slice(h * HEAD, (h + 1) * HEAD)
        qa[:, cut] = head_norm(acc[:, cut], qg[:1]).astype(BF16)
    own[...] = qa[:, head_slice(idx, 0)]
    next_[...] = qa[:, head_slice(idx, 1)]
    for j in range(2):
        other[j] = qa[:, head_slice(idx, 2 + j)]


def project_queries(idx, xs, wq, gain):
    return pl.pallas_call(
        query_kernel,
        out_shape=[
            jax.ShapeDtypeStruct((ROWS, HEAD), BF16),
            jax.ShapeDtypeStruct((ROWS, HEAD), BF16),
            jax.ShapeDtypeStruct((2, ROWS, HEAD), BF16),
            jax.ShapeDtypeStruct((ROWS, COLS), BF16),
            jax.ShapeDtypeStruct((4, ROWS, PART), BF16),
        ],
        in_specs=[smem()] + vmem(5) + hbm(1) + vmem(1),
        out_specs=vmem(5),
        scratch_shapes=[pltpu.VMEM((4, PART, COLS), BF16), pltpu.SemaphoreType.DMA((4,))],
        compiler_params=params(50),
        cost_estimate=pl.CostEstimate(
            flops=2 * ROWS * WIDTH * COLS, bytes_accessed=5 << 20, transcendentals=0
        ),
        name="queries",
    )(idx, *xs, wq, gain)


def fresh_kernel(idx, xs, qa, wk, wv, kg, _, fk, fv, out, lse):
    acc = project(idx, xs, wk)
    for h in range(4):
        cut = slice(h * HEAD, (h + 1) * HEAD)
        fk[:, cut] = head_norm(acc[:, cut], kg[1:]).astype(BF16)
    fv[...] = project(idx, xs, wv).astype(BF16)
    shape = (ROWS, ROWS)
    row_image = lax.broadcasted_iota(jnp.int32, shape, 0) // TOK
    col_image = lax.broadcasted_iota(jnp.int32, shape, 1) // TOK
    lanes = lax.broadcasted_iota(jnp.int32, (ROWS, HEAD), 1)
    levels = jnp.zeros((ROWS, HEAD), F32)
    for h in range(4):
        cut = slice(h * HEAD, (h + 1) * HEAD)
        s = dot_t(qa[:, cut], fk[:, cut]) * SCORE
        s = jnp.where(row_image == col_image, s, -1e30)
        top = jnp.max(s, axis=-1, keepdims=True)
        p = jnp.exp2(s - top)
        total = jnp.sum(p, axis=-1, keepdims=True)
        numer = jnp.dot(p.astype(BF16), fv[:, cut], preferred_element_type=F32)
        out[:, cut] = numer / total
        levels = jnp.where(lanes == h, top + jnp.log2(total), levels)
    lse[...] = levels


def fresh(idx, xs, qa, wk, wv, gain, dep):
    return pl.pallas_call(
        fresh_kernel,
        out_shape=[jax.ShapeDtypeStruct((ROWS, COLS), BF16)] * 2
        + [
            jax.ShapeDtypeStruct((ROWS, COLS), F32),
            jax.ShapeDtypeStruct((ROWS, HEAD), F32),
        ],
        in_specs=[smem()] + vmem(5) + anywhere(1),
        out_specs=vmem(4),
        compiler_params=params(16),
        cost_estimate=pl.CostEstimate(
            flops=4 * ROWS * WIDTH * COLS, bytes_accessed=9 << 20, transcendentals=0
        ),
        name="fresh",
    )(idx, xs, qa, wk, wv, gain, dep)


def attend_part(q, stream, state, mask):
    entries = 16
    count = entries * TOK
    for c in range(stream.shape[0] // entries):
        span = slice(c * entries, (c + 1) * entries)
        k = stream[span, 0].reshape(count, HEAD)
        v = stream[span, 1].reshape(count, HEAD)
        s = dot_t(q, k) * SCORE
        if state is None:
            s = jnp.concatenate(
                [jnp.where(mask, -1e30, s[:, : 4 * TOK]), s[:, 4 * TOK :]], axis=1
            )
            top = jnp.max(s, axis=-1, keepdims=True)
            p = jnp.exp2(s - top)
            total = jnp.sum(p, axis=-1, keepdims=True)
            numer = jnp.dot(p.astype(BF16), v, preferred_element_type=F32)
        else:
            old, total, numer = state
            top = jnp.maximum(old, jnp.max(s, axis=-1, keepdims=True))
            factor = jnp.exp2(old - top)
            p = jnp.exp2(s - top)
            total = total * factor + jnp.sum(p, axis=-1, keepdims=True)
            numer = numer * factor + jnp.dot(p.astype(BF16), v, preferred_element_type=F32)
        state = (top, total, numer)
    return state


def attend_kernel(number, first_patch, *refs):
    groups, (s0, t0, s1, t1) = refs[:number], refs[number : number + 4]
    outs = refs[-number:]
    count = 2 * len(groups)
    shape = (count * TOK, 4 * TOK)
    row_patch = lax.broadcasted_iota(jnp.int32, shape, 0) // TOK + first_patch
    col_patch = lax.broadcasted_iota(jnp.int32, shape, 1) // TOK
    lse_rows = [jnp.zeros((1, HEAD), F32) for _ in range(count)]
    row = lax.broadcasted_iota(jnp.int32, (TOK, HEAD), 0)
    lane = lax.broadcasted_iota(jnp.int32, (TOK, HEAD), 1)
    for i, streams in enumerate(((s0, t0), (s1, t1))):
        q = jnp.concatenate(
            [r[j, i * TOK : (i + 1) * TOK] for r in groups for j in range(2)], axis=0
        )
        state = None
        for stream in streams:
            state = attend_part(q, stream, state, row_patch == col_patch)
        top, total, numer = state
        out = (numer / total).astype(BF16)
        level = top + jnp.log2(total)
        for d in range(count):
            span = slice(d * TOK, (d + 1) * TOK)
            outs[d // 2][d % 2, i * TOK : (i + 1) * TOK, :] = out[span]
            lse_rows[d] += jnp.sum(
                jnp.where(lane == row + i * TOK, level[span], 0.0), axis=0, keepdims=True
            )
    sub = lax.broadcasted_iota(jnp.int32, (16, HEAD), 0)
    for d in range(count):
        high = lse_rows[d].astype(BF16).astype(F32)
        rest = lse_rows[d] - high
        middle = rest.astype(BF16).astype(F32)
        low = rest - middle
        tail = jnp.where(sub == 0, high, jnp.where(sub == 1, middle, jnp.where(sub == 2, low, 0.0)))
        outs[d // 2][d % 2, ROWS : ROWS + 16, :] = tail.astype(BF16)


def attend(groups, streams, first_patch, deps=()):
    number = len(groups)
    return pl.pallas_call(
        functools.partial(attend_kernel, number, first_patch),
        out_shape=[jax.ShapeDtypeStruct((2, ROWS + 16, HEAD), BF16)] * number,
        in_specs=vmem(number + 4) + anywhere(len(deps)),
        out_specs=vmem(number),
        compiler_params=params(32),
        cost_estimate=pl.CostEstimate(
            flops=2 * number << 30, bytes_accessed=8 << 20, transcendentals=1 << 22
        ),
        name="attend",
    )(*groups, *streams, *deps)


def combine_kernel(heads, g, z, y, d, other, near_out, near_lse, att):
    row = lax.broadcasted_iota(jnp.int32, (ROWS, HEAD), 0)
    lane = lax.broadcasted_iota(jnp.int32, (ROWS, HEAD), 1)
    halves = ((g.at[0], z.at[0]), (y.at[0], d.at[0]), (other.at[0], other.at[1]),
              (other.at[2], other.at[3]))
    for h, pair in enumerate(halves):
        cut = head_slice(heads, h)
        levels = [
            jnp.sum(jnp.where(lane == head_of(heads, h), near_lse[...], 0.0), axis=1, keepdims=True)
        ]
        parts = [near_out[:, cut]]
        for r in pair:
            tail = r[ROWS : ROWS + 16, :].astype(F32)
            level = tail[0:1] + tail[1:2] + tail[2:3]
            levels.append(jnp.sum(jnp.where(lane == row, level, 0.0), axis=1, keepdims=True))
            parts.append(r[:ROWS, :].astype(F32))
        top = jnp.maximum(jnp.maximum(levels[0], levels[1]), levels[2])
        weights = [jnp.exp2(level - top) for level in levels]
        out = sum(w * p for w, p in zip(weights, parts))
        att[:, cut] = (out / sum(weights)).astype(BF16)


def combine(heads, parts, near_out, near_lse):
    return pl.pallas_call(
        combine_kernel,
        out_shape=jax.ShapeDtypeStruct((ROWS, COLS), BF16),
        in_specs=[smem()] + vmem(7),
        out_specs=pl.BlockSpec(memory_space=pltpu.VMEM),
        compiler_params=params(8),
        name="combine",
    )(heads, *parts, near_out, near_lse)


def swap(value, axis, step):
    flips = ((1, 3), (3, 1))[step]
    if axis == "zh":
        names, far, near_ = ("core", axis), 1, 4
    else:
        names, far, near_ = (axis, "core"), 2, 1
    perm = [
        (a * far + c * near_, (a ^ flips[c]) * far + c * near_)
        for a in range(4)
        for c in range(2)
    ]
    return lax.ppermute(value, names, perm)


def diagonal(value):
    perm = [
        (z * 8 + y * 2 + c, (z ^ 1) * 8 + (y ^ (1, 3)[c]) * 2 + c)
        for z in range(2)
        for y in range(4)
        for c in range(2)
    ]
    return lax.ppermute(value, ("zl", "y", "core"), perm)


def on_device(activations, mod_shift, mod_scale, w_query, w_key, w_value,
              query_gain, key_gain, stale_keys, stale_values):
    code = lax.axis_index("zh") * 8 + lax.axis_index("y") * 2 + lax.axis_index("core")
    code = code.astype(jnp.int32).reshape(1)

    own, next_, other, x0 = pack(
        code, stale_keys, stale_values, activations.reshape(ROWS, PART), mod_shift, mod_scale
    )
    x1 = swap(x0, "zh", 0)
    x2 = swap(activations.reshape(ROWS, PART), "zh", 1)
    other = lax.ppermute(other, "core", FLIP)
    shape = (IMG, 2, TOK, HEAD)
    (far,) = call(pair_kernel, "pair", 8, [(2,) + shape], (next_, other))
    far = swap(far, "y", 0)
    gains = (query_gain.reshape(1, HEAD), key_gain.reshape(1, HEAD))
    x0, own, gains = hold(x0, own, gains)
    s0, s1 = call(
        stack_kernel, "stack", 8, [(4,) + shape[1:]] * 2, (own, other, far), (gains,)
    )
    s0, s1 = join([(s0, swap(s0, "y", 1)), (s1, swap(s1, "x", 0))], (x1, x2))
    x3 = swap(x1, "zh", 1)
    (m2,) = call(mods_kernel, "mods", 8, [(16, PART)], (x1,))
    m2 = lax.ppermute(m2, "core", FLIP)
    own, next_, other, qa, xs = project_queries(
        code, (x0, x1, x2, x3, m2), w_query, gains
    )
    s0, s1 = join([(s0, swap(s0, "x", 0)), (s1, swap(s1, "x", 1))], (own,))
    t0, t1 = swap(s0, "x", 1), swap(s1, "y", 1)

    other = lax.ppermute(other, "core", FLIP)
    g, n = call(query_pairs_kernel, "query_pairs", 8, [(2, ROWS, HEAD)] * 2, (own, next_, other))
    groups = (swap(n, "y", 0), lax.ppermute(g, "zl", FLIP), diagonal(n))
    streams = (s0, t0, s1, t1)
    py, pz, pd = attend(groups, streams, 2)
    (pg,) = attend((g,), streams, 0, (py,))
    fk, fv, near_out, near_lse = fresh(
        code, xs, qa, w_key, w_value, gains, py
    )
    py, pz, pd = swap(py, "y", 0), lax.ppermute(pz, "zl", FLIP), diagonal(pd)
    (back,) = call(
        back_kernel, "back", 8, [(4, ROWS + 16, HEAD)], (pg, py, pz, pd), (near_lse,)
    )
    back = lax.ppermute(back, "core", FLIP)
    att = combine(code, (pg, pz, py, pd, back), near_out, near_lse)
    shape = (IMG, TOK, COLS)
    return att.reshape(shape), fk.reshape(shape), fv.reshape(shape)


def solution(mesh):
    split = Mesh(mesh.devices.reshape(4, 2, 4, 2, 4), ("x", "zl", "y", "core", "zh"))
    patch = ("x", "zl", "y", "core")
    rows = P(None, patch, "zh")
    cols = P(None, "zh")
    return jax.shard_map(
        on_device,
        mesh=split,
        in_specs=(rows, cols, cols, cols, cols, cols, P(), P(), rows, rows),
        out_specs=(rows, rows, rows),
        check_vma=False,
    )
```

```python
import functools
import math

import jax
import jax.numpy as jnp
from jax import lax
from jax.experimental import pallas as pl
from jax.experimental.pallas import tpu as pltpu
from jax.sharding import Mesh, PartitionSpec as P

HEAD = 128
TOK = 64
IMG = 2
WIDTH = 4096
PART = 1024
COLS = 512
ROWS = IMG * TOK
SCORE = math.log2(math.e) / math.sqrt(HEAD)
F32 = jnp.float32
BF16 = jnp.bfloat16
FLIP = [(0, 1), (1, 0)]


def params(limit):
    return pltpu.CompilerParams(vmem_limit_bytes=limit * 1024 * 1024)


def vmem(count):
    return [pl.BlockSpec(memory_space=pltpu.VMEM)] * count


def hbm(count):
    return [pl.BlockSpec(memory_space=pltpu.HBM)] * count


def anywhere(count):
    return [pl.BlockSpec(memory_space=pl.ANY)] * count


def smem():
    return pl.BlockSpec(memory_space=pltpu.SMEM)


def dot_t(a, b):
    return lax.dot_general(a, b, (((1,), (1,)), ((), ())), preferred_element_type=F32)


def head_of(code, d):
    core, y = code[0] & 1, (code[0] >> 1) & 3
    side = core ^ (d >> 1)
    bit = jnp.where(side == 0, (y ^ (y >> 1)) & 1, y >> 1)
    return 2 * side + (bit ^ (d & 1))


def head_slice(code, d):
    return pl.ds(pl.multiple_of(head_of(code, d) * HEAD, HEAD), HEAD)


def rank_of(code, j):
    flips = (0, jnp.where(code[0] & 1 == 0, 1, 3), jnp.where(code[0] & 1 == 0, 3, 1), 2)
    return (code[0] >> 3) ^ flips[j]


def pack_kernel(heads, keys, values, x, shift, scale, own, next_, other, pay, mods, sems):
    copies = []

    def copy(source, target):
        copies.append(pltpu.make_async_copy(source, target, sems.at[len(copies)]))
        copies[-1].start()

    copy(shift, mods.at[0])
    copy(scale, mods.at[1])
    copy(x, pay.at[:ROWS])
    for d, out in ((2, other.at[0]), (3, other.at[1]), (1, next_), (0, own)):
        cut = head_slice(heads, d)
        for i in range(IMG):
            for j, source in enumerate((keys, values)):
                copy(source.at[i, :, cut], out.at[i, j])
    for one in copies[:2]:
        one.wait()
    pay[ROWS:] = jnp.zeros((16, PART), BF16)
    pay[ROWS : ROWS + IMG] = mods[0]
    pay[ROWS + IMG : ROWS + 2 * IMG] = mods[1]
    for one in copies[2:]:
        one.wait()


def pack(heads, keys, values, x, shift, scale):
    shape = (IMG, 2, TOK, HEAD)
    return pl.pallas_call(
        pack_kernel,
        out_shape=[
            jax.ShapeDtypeStruct(shape, BF16),
            jax.ShapeDtypeStruct(shape, BF16),
            jax.ShapeDtypeStruct((2,) + shape, BF16),
            jax.ShapeDtypeStruct((ROWS + 16, PART), BF16),
        ],
        in_specs=[smem()] + hbm(5),
        out_specs=vmem(4),
        scratch_shapes=[pltpu.VMEM((2, IMG, PART), BF16), pltpu.SemaphoreType.DMA((19,))],
        compiler_params=params(56),
        name="pack",
    )(heads, keys, values, x, shift, scale)


def call(kernel, name, limit, shapes, operands, deps=(), cost=None):
    return pl.pallas_call(
        kernel,
        out_shape=[jax.ShapeDtypeStruct(s, BF16) for s in shapes],
        in_specs=vmem(len(operands)) + anywhere(len(deps)),
        out_specs=vmem(len(shapes)),
        compiler_params=params(limit),
        cost_estimate=cost,
        name=name,
    )(*operands, *deps)


def join(groups, deps=()):
    counts = [len(g) for g in groups]

    def kernel(*refs):
        ins, outs = refs[: sum(counts)], refs[sum(counts) + len(deps) :]
        at = 0
        for out, count in zip(outs, counts):
            row = 0
            for r in ins[at : at + count]:
                out[row : row + r.shape[0]] = r[...]
                row += r.shape[0]
            at += count

    def shape(group):
        rows = sum(v.shape[0] for v in group)
        return jax.ShapeDtypeStruct((rows,) + group[0].shape[1:], group[0].dtype)

    return pl.pallas_call(
        kernel,
        out_shape=[shape(g) for g in groups],
        in_specs=vmem(sum(counts)) + anywhere(len(deps)),
        out_specs=vmem(len(groups)),
        compiler_params=params(12),
        name="join",
    )(*[v for g in groups for v in g], *deps)


def hold(x0, own, gains):
    def kernel(x_in, own_in, qg, kg, x_out, own_out, gains_out):
        x_out[...] = x_in[...]
        own_out[...] = own_in[...]
        gains_out[:1] = qg[...]
        gains_out[1:] = kg[...]

    return pl.pallas_call(
        kernel,
        out_shape=[
            jax.ShapeDtypeStruct(x0.shape, BF16),
            jax.ShapeDtypeStruct(own.shape, BF16),
            jax.ShapeDtypeStruct((2, HEAD), F32),
        ],
        in_specs=vmem(4),
        out_specs=vmem(3),
        compiler_params=params(8),
        cost_estimate=pl.CostEstimate(flops=0, bytes_accessed=32 << 20, transcendentals=0),
        name="hold",
    )(x0, own, *gains)


def mods_kernel(x, out):
    out[...] = x[ROWS:]


def pair_kernel(a, b, out):
    out[0] = a[...]
    out[1] = b[1]


def stack_kernel(own, other, far, _, s0, s1):
    for i, s in enumerate((s0, s1)):
        s[0] = own[i]
        s[1] = other[0, i]
        s[2] = far[0, i]
        s[3] = far[1, i]


def query_pairs_kernel(own, next_, other, g, n):
    g[0] = own[...]
    g[1] = other[0]
    n[0] = next_[...]
    n[1] = other[1]


def back_kernel(g, y, z, d, _, out):
    for j, r in enumerate((g, z, y, d)):
        out[j] = r[1]


def project(code, xs, w):
    acc = jnp.zeros((ROWS, COLS), F32)
    for j in range(4):
        rows = pl.ds(pl.multiple_of(rank_of(code, j) * PART, PART), PART)
        acc += jnp.dot(xs[j], w[rows, :], preferred_element_type=F32)
    return acc


def head_norm(v, gain):
    return v * lax.rsqrt(jnp.mean(v * v, axis=-1, keepdims=True) + 1e-06) * gain


def query_kernel(idx, x0, x1, x2, x3, m2, wq, qg, own, next_, other, qa, xs):
    blocks = (x0, x1, x2, x3)
    total = sum(jnp.sum(b[:ROWS].astype(F32), axis=-1, keepdims=True) for b in blocks)
    mean = total / WIDTH
    square = jnp.zeros_like(mean)
    for b in blocks:
        centred = b[:ROWS].astype(F32) - mean
        square += jnp.sum(centred * centred, axis=-1, keepdims=True)
    rstd = lax.rsqrt(square / WIDTH + 1e-06)
    for j, b in enumerate(blocks):
        mods = (m2[...] if j == 2 else b[ROWS : ROWS + 16]).astype(F32)
        for i in range(IMG):
            rows = slice(i * TOK, (i + 1) * TOK)
            normed = (b[rows].astype(F32) - mean[rows]) * rstd[rows]
            out = normed * (1.0 + mods[IMG + i : IMG + i + 1, :]) + mods[i : i + 1, :]
            xs[j, rows, :] = out.astype(BF16)
    acc = project(idx, xs, wq)
    for h in range(4):
        cut = slice(h * HEAD, (h + 1) * HEAD)
        qa[:, cut] = head_norm(acc[:, cut], qg[:1]).astype(BF16)
    own[...] = qa[:, head_slice(idx, 0)]
    next_[...] = qa[:, head_slice(idx, 1)]
    for j in range(2):
        other[j] = qa[:, head_slice(idx, 2 + j)]


def project_queries(idx, xs, wq, gain):
    return pl.pallas_call(
        query_kernel,
        out_shape=[
            jax.ShapeDtypeStruct((ROWS, HEAD), BF16),
            jax.ShapeDtypeStruct((ROWS, HEAD), BF16),
            jax.ShapeDtypeStruct((2, ROWS, HEAD), BF16),
            jax.ShapeDtypeStruct((ROWS, COLS), BF16),
            jax.ShapeDtypeStruct((4, ROWS, PART), BF16),
        ],
        in_specs=[smem()] + vmem(7),
        out_specs=vmem(5),
        compiler_params=params(16),
        cost_estimate=pl.CostEstimate(
            flops=2 * ROWS * WIDTH * COLS, bytes_accessed=5 << 20, transcendentals=0
        ),
        name="queries",
    )(idx, *xs, wq, gain)


def fresh_kernel(idx, xs, qa, wk, wv, kg, _, fk, fv, out, lse):
    acc = project(idx, xs, wk)
    for h in range(4):
        cut = slice(h * HEAD, (h + 1) * HEAD)
        fk[:, cut] = head_norm(acc[:, cut], kg[1:]).astype(BF16)
    fv[...] = project(idx, xs, wv).astype(BF16)
    shape = (ROWS, ROWS)
    row_image = lax.broadcasted_iota(jnp.int32, shape, 0) // TOK
    col_image = lax.broadcasted_iota(jnp.int32, shape, 1) // TOK
    lanes = lax.broadcasted_iota(jnp.int32, (ROWS, HEAD), 1)
    levels = jnp.zeros((ROWS, HEAD), F32)
    for h in range(4):
        cut = slice(h * HEAD, (h + 1) * HEAD)
        s = dot_t(qa[:, cut], fk[:, cut]) * SCORE
        s = jnp.where(row_image == col_image, s, -1e30)
        top = jnp.max(s, axis=-1, keepdims=True)
        p = jnp.exp2(s - top)
        total = jnp.sum(p, axis=-1, keepdims=True)
        numer = jnp.dot(p.astype(BF16), fv[:, cut], preferred_element_type=F32)
        out[:, cut] = numer / total
        levels = jnp.where(lanes == h, top + jnp.log2(total), levels)
    lse[...] = levels


def fresh(idx, xs, qa, wk, wv, gain, dep):
    return pl.pallas_call(
        fresh_kernel,
        out_shape=[jax.ShapeDtypeStruct((ROWS, COLS), BF16)] * 2
        + [
            jax.ShapeDtypeStruct((ROWS, COLS), F32),
            jax.ShapeDtypeStruct((ROWS, HEAD), F32),
        ],
        in_specs=[smem()] + vmem(5) + anywhere(1),
        out_specs=vmem(4),
        compiler_params=params(16),
        cost_estimate=pl.CostEstimate(
            flops=4 * ROWS * WIDTH * COLS, bytes_accessed=9 << 20, transcendentals=0
        ),
        name="fresh",
    )(idx, xs, qa, wk, wv, gain, dep)


def attend_part(q, stream, state, mask):
    entries = 16
    count = entries * TOK
    for c in range(stream.shape[0] // entries):
        span = slice(c * entries, (c + 1) * entries)
        k = stream[span, 0].reshape(count, HEAD)
        v = stream[span, 1].reshape(count, HEAD)
        s = dot_t(q, k) * SCORE
        if state is None:
            s = jnp.concatenate(
                [jnp.where(mask, -1e30, s[:, : 4 * TOK]), s[:, 4 * TOK :]], axis=1
            )
            top = jnp.max(s, axis=-1, keepdims=True)
            p = jnp.exp2(s - top)
            total = jnp.sum(p, axis=-1, keepdims=True)
            numer = jnp.dot(p.astype(BF16), v, preferred_element_type=F32)
        else:
            old, total, numer = state
            top = jnp.maximum(old, jnp.max(s, axis=-1, keepdims=True))
            factor = jnp.exp2(old - top)
            p = jnp.exp2(s - top)
            total = total * factor + jnp.sum(p, axis=-1, keepdims=True)
            numer = numer * factor + jnp.dot(p.astype(BF16), v, preferred_element_type=F32)
        state = (top, total, numer)
    return state


def attend_kernel(number, first_patch, *refs):
    groups, (s0, t0, s1, t1) = refs[:number], refs[number : number + 4]
    outs = refs[-number:]
    count = 2 * len(groups)
    shape = (count * TOK, 4 * TOK)
    row_patch = lax.broadcasted_iota(jnp.int32, shape, 0) // TOK + first_patch
    col_patch = lax.broadcasted_iota(jnp.int32, shape, 1) // TOK
    lse_rows = [jnp.zeros((1, HEAD), F32) for _ in range(count)]
    row = lax.broadcasted_iota(jnp.int32, (TOK, HEAD), 0)
    lane = lax.broadcasted_iota(jnp.int32, (TOK, HEAD), 1)
    for i, streams in enumerate(((s0, t0), (s1, t1))):
        q = jnp.concatenate(
            [r[j, i * TOK : (i + 1) * TOK] for r in groups for j in range(2)], axis=0
        )
        state = None
        for stream in streams:
            state = attend_part(q, stream, state, row_patch == col_patch)
        top, total, numer = state
        out = (numer / total).astype(BF16)
        level = top + jnp.log2(total)
        for d in range(count):
            span = slice(d * TOK, (d + 1) * TOK)
            outs[d // 2][d % 2, i * TOK : (i + 1) * TOK, :] = out[span]
            lse_rows[d] += jnp.sum(
                jnp.where(lane == row + i * TOK, level[span], 0.0), axis=0, keepdims=True
            )
    sub = lax.broadcasted_iota(jnp.int32, (16, HEAD), 0)
    for d in range(count):
        high = lse_rows[d].astype(BF16).astype(F32)
        rest = lse_rows[d] - high
        middle = rest.astype(BF16).astype(F32)
        low = rest - middle
        tail = jnp.where(sub == 0, high, jnp.where(sub == 1, middle, jnp.where(sub == 2, low, 0.0)))
        outs[d // 2][d % 2, ROWS : ROWS + 16, :] = tail.astype(BF16)


def attend(groups, streams, first_patch, deps=()):
    number = len(groups)
    return pl.pallas_call(
        functools.partial(attend_kernel, number, first_patch),
        out_shape=[jax.ShapeDtypeStruct((2, ROWS + 16, HEAD), BF16)] * number,
        in_specs=vmem(number + 4) + anywhere(len(deps)),
        out_specs=vmem(number),
        compiler_params=params(32),
        cost_estimate=pl.CostEstimate(
            flops=2 * number << 30, bytes_accessed=8 << 20, transcendentals=1 << 22
        ),
        name="attend",
    )(*groups, *streams, *deps)


def combine_kernel(heads, g, z, y, d, other, near_out, near_lse, att):
    row = lax.broadcasted_iota(jnp.int32, (ROWS, HEAD), 0)
    lane = lax.broadcasted_iota(jnp.int32, (ROWS, HEAD), 1)
    halves = ((g.at[0], z.at[0]), (y.at[0], d.at[0]), (other.at[0], other.at[1]),
              (other.at[2], other.at[3]))
    for h, pair in enumerate(halves):
        cut = head_slice(heads, h)
        levels = [
            jnp.sum(jnp.where(lane == head_of(heads, h), near_lse[...], 0.0), axis=1, keepdims=True)
        ]
        parts = [near_out[:, cut]]
        for r in pair:
            tail = r[ROWS : ROWS + 16, :].astype(F32)
            level = tail[0:1] + tail[1:2] + tail[2:3]
            levels.append(jnp.sum(jnp.where(lane == row, level, 0.0), axis=1, keepdims=True))
            parts.append(r[:ROWS, :].astype(F32))
        top = jnp.maximum(jnp.maximum(levels[0], levels[1]), levels[2])
        weights = [jnp.exp2(level - top) for level in levels]
        out = sum(w * p for w, p in zip(weights, parts))
        att[:, cut] = (out / sum(weights)).astype(BF16)


def combine(heads, parts, near_out, near_lse):
    return pl.pallas_call(
        combine_kernel,
        out_shape=jax.ShapeDtypeStruct((ROWS, COLS), BF16),
        in_specs=[smem()] + vmem(7),
        out_specs=pl.BlockSpec(memory_space=pltpu.VMEM),
        compiler_params=params(8),
        name="combine",
    )(heads, *parts, near_out, near_lse)


def swap(value, axis, step):
    flips = ((1, 3), (3, 1))[step]
    if axis == "zh":
        names, far, near_ = ("core", axis), 1, 4
    else:
        names, far, near_ = (axis, "core"), 2, 1
    perm = [
        (a * far + c * near_, (a ^ flips[c]) * far + c * near_)
        for a in range(4)
        for c in range(2)
    ]
    return lax.ppermute(value, names, perm)


def diagonal(value):
    perm = [
        (z * 8 + y * 2 + c, (z ^ 1) * 8 + (y ^ (1, 3)[c]) * 2 + c)
        for z in range(2)
        for y in range(4)
        for c in range(2)
    ]
    return lax.ppermute(value, ("zl", "y", "core"), perm)


def on_device(activations, mod_shift, mod_scale, w_query, w_key, w_value,
              query_gain, key_gain, stale_keys, stale_values):
    code = lax.axis_index("zh") * 8 + lax.axis_index("y") * 2 + lax.axis_index("core")
    code = code.astype(jnp.int32).reshape(1)

    own, next_, other, x0 = pack(
        code, stale_keys, stale_values, activations.reshape(ROWS, PART), mod_shift, mod_scale
    )
    x1 = swap(x0, "zh", 0)
    x2 = swap(activations.reshape(ROWS, PART), "zh", 1)
    other = lax.ppermute(other, "core", FLIP)
    shape = (IMG, 2, TOK, HEAD)
    (far,) = call(pair_kernel, "pair", 8, [(2,) + shape], (next_, other))
    far = swap(far, "y", 0)
    gains = (query_gain.reshape(1, HEAD), key_gain.reshape(1, HEAD))
    x0, own, gains = hold(x0, own, gains)
    s0, s1 = call(
        stack_kernel, "stack", 8, [(4,) + shape[1:]] * 2, (own, other, far), (gains,)
    )
    s0, s1 = join([(s0, swap(s0, "y", 1)), (s1, swap(s1, "x", 0))], (x1, x2))
    x3 = swap(x1, "zh", 1)
    cost = pl.CostEstimate(flops=8 << 30, bytes_accessed=1 << 20, transcendentals=0)
    (m2,) = call(mods_kernel, "mods", 8, [(16, PART)], (x1,), (), cost)
    m2 = lax.ppermute(m2, "core", FLIP)
    own, next_, other, qa, xs = project_queries(
        code, (x0, x1, x2, x3, m2), w_query, gains
    )
    s0, s1 = join([(s0, swap(s0, "x", 0)), (s1, swap(s1, "x", 1))], (own,))
    t0, t1 = swap(s0, "x", 1), swap(s1, "y", 1)

    other = lax.ppermute(other, "core", FLIP)
    cost = pl.CostEstimate(flops=8 << 30, bytes_accessed=1 << 20, transcendentals=0)
    g, n = call(
        query_pairs_kernel, "query_pairs", 8, [(2, ROWS, HEAD)] * 2, (own, next_, other), (), cost
    )
    groups = (swap(n, "y", 0), lax.ppermute(g, "zl", FLIP), diagonal(n))
    streams = (s0, t0, s1, t1)
    py, pz, pd = attend(groups, streams, 2)
    (pg,) = attend((g,), streams, 0, (py,))
    fk, fv, near_out, near_lse = fresh(
        code, xs, qa, w_key, w_value, gains, py
    )
    py, pz, pd = swap(py, "y", 0), lax.ppermute(pz, "zl", FLIP), diagonal(pd)
    (back,) = call(
        back_kernel, "back", 8, [(4, ROWS + 16, HEAD)], (pg, py, pz, pd), (near_lse,)
    )
    back = lax.ppermute(back, "core", FLIP)
    att = combine(code, (pg, pz, py, pd, back), near_out, near_lse)
    shape = (IMG, TOK, COLS)
    return att.reshape(shape), fk.reshape(shape), fv.reshape(shape)


def solution(mesh):
    split = Mesh(mesh.devices.reshape(4, 2, 4, 2, 4), ("x", "zl", "y", "core", "zh"))
    patch = ("x", "zl", "y", "core")
    rows = P(None, patch, "zh")
    cols = P(None, "zh")
    return jax.shard_map(
        on_device,
        mesh=split,
        in_specs=(rows, cols, cols, cols, cols, cols, P(), P(), rows, rows),
        out_specs=(rows, rows, rows),
        check_vma=False,
    )
```

```python
import functools
import math

import jax
import jax.numpy as jnp
from jax import lax
from jax.experimental import pallas as pl
from jax.experimental.pallas import tpu as pltpu
from jax.sharding import Mesh, PartitionSpec as P

HEAD = 128
TOK = 64
IMG = 2
WIDTH = 4096
PART = 1024
COLS = 512
ROWS = IMG * TOK
SCORE = math.log2(math.e) / math.sqrt(HEAD)
F32 = jnp.float32
BF16 = jnp.bfloat16
FLIP = [(0, 1), (1, 0)]


def params(limit):
    return pltpu.CompilerParams(vmem_limit_bytes=limit * 1024 * 1024)


def vmem(count):
    return [pl.BlockSpec(memory_space=pltpu.VMEM)] * count


def hbm(count):
    return [pl.BlockSpec(memory_space=pltpu.HBM)] * count


def anywhere(count):
    return [pl.BlockSpec(memory_space=pl.ANY)] * count


def smem():
    return pl.BlockSpec(memory_space=pltpu.SMEM)


def dot_t(a, b):
    return lax.dot_general(a, b, (((1,), (1,)), ((), ())), preferred_element_type=F32)


def head_of(code, d):
    core, y = code[0] & 1, (code[0] >> 1) & 3
    side = core ^ (d >> 1)
    bit = jnp.where(side == 0, (y ^ (y >> 1)) & 1, y >> 1)
    return 2 * side + (bit ^ (d & 1))


def head_slice(code, d):
    return pl.ds(pl.multiple_of(head_of(code, d) * HEAD, HEAD), HEAD)


def rank_of(code, j):
    flips = (0, jnp.where(code[0] & 1 == 0, 1, 3), jnp.where(code[0] & 1 == 0, 3, 1), 2)
    return (code[0] >> 3) ^ flips[j]


def pack_kernel(heads, keys, values, x, shift, scale, own, next_, other, pay, mods, sems):
    copies = []

    def copy(source, target):
        copies.append(pltpu.make_async_copy(source, target, sems.at[len(copies)]))
        copies[-1].start()

    copy(shift, mods.at[0])
    copy(scale, mods.at[1])
    copy(x, pay.at[:ROWS])
    for d, out in ((2, other.at[0]), (3, other.at[1]), (1, next_), (0, own)):
        cut = head_slice(heads, d)
        for i in range(IMG):
            for j, source in enumerate((keys, values)):
                copy(source.at[i, :, cut], out.at[i, j])
    for one in copies[:2]:
        one.wait()
    pay[ROWS:] = jnp.zeros((16, PART), BF16)
    pay[ROWS : ROWS + IMG] = mods[0]
    pay[ROWS + IMG : ROWS + 2 * IMG] = mods[1]
    for one in copies[2:]:
        one.wait()


def pack(heads, keys, values, x, shift, scale):
    shape = (IMG, 2, TOK, HEAD)
    return pl.pallas_call(
        pack_kernel,
        out_shape=[
            jax.ShapeDtypeStruct(shape, BF16),
            jax.ShapeDtypeStruct(shape, BF16),
            jax.ShapeDtypeStruct((2,) + shape, BF16),
            jax.ShapeDtypeStruct((ROWS + 16, PART), BF16),
        ],
        in_specs=[smem()] + hbm(5),
        out_specs=vmem(4),
        scratch_shapes=[pltpu.VMEM((2, IMG, PART), BF16), pltpu.SemaphoreType.DMA((19,))],
        compiler_params=params(56),
        name="pack",
    )(heads, keys, values, x, shift, scale)


def call(kernel, name, limit, shapes, operands, deps=(), cost=None):
    return pl.pallas_call(
        kernel,
        out_shape=[jax.ShapeDtypeStruct(s, BF16) for s in shapes],
        in_specs=vmem(len(operands)) + anywhere(len(deps)),
        out_specs=vmem(len(shapes)),
        compiler_params=params(limit),
        cost_estimate=cost,
        name=name,
    )(*operands, *deps)


def join(groups, deps=()):
    counts = [len(g) for g in groups]

    def kernel(*refs):
        ins, outs = refs[: sum(counts)], refs[sum(counts) + len(deps) :]
        at = 0
        for out, count in zip(outs, counts):
            row = 0
            for r in ins[at : at + count]:
                out[row : row + r.shape[0]] = r[...]
                row += r.shape[0]
            at += count

    def shape(group):
        rows = sum(v.shape[0] for v in group)
        return jax.ShapeDtypeStruct((rows,) + group[0].shape[1:], group[0].dtype)

    return pl.pallas_call(
        kernel,
        out_shape=[shape(g) for g in groups],
        in_specs=vmem(sum(counts)) + anywhere(len(deps)),
        out_specs=vmem(len(groups)),
        compiler_params=params(12),
        name="join",
    )(*[v for g in groups for v in g], *deps)


def hold(x0, own, gains):
    def kernel(x_in, own_in, qg, kg, x_out, own_out, gains_out):
        x_out[...] = x_in[...]
        own_out[...] = own_in[...]
        gains_out[:1] = qg[...]
        gains_out[1:] = kg[...]

    return pl.pallas_call(
        kernel,
        out_shape=[
            jax.ShapeDtypeStruct(x0.shape, BF16),
            jax.ShapeDtypeStruct(own.shape, BF16),
            jax.ShapeDtypeStruct((2, HEAD), F32),
        ],
        in_specs=vmem(4),
        out_specs=vmem(3),
        compiler_params=params(8),
        cost_estimate=pl.CostEstimate(flops=0, bytes_accessed=32 << 20, transcendentals=0),
        name="hold",
    )(x0, own, *gains)


def mark(dep):
    def kernel(_, out):
        out[...] = jnp.zeros_like(out)

    return pl.pallas_call(
        kernel,
        out_shape=jax.ShapeDtypeStruct((8, HEAD), F32),
        in_specs=anywhere(1),
        out_specs=pl.BlockSpec(memory_space=pltpu.VMEM),
        compiler_params=params(4),
        cost_estimate=pl.CostEstimate(flops=4 << 30, bytes_accessed=4096, transcendentals=0),
        name="mark",
    )(dep)


def mods_kernel(x, out):
    out[...] = x[ROWS:]


def pair_kernel(a, b, out):
    out[0] = a[...]
    out[1] = b[1]


def stack_kernel(own, other, far, _, s0, s1):
    for i, s in enumerate((s0, s1)):
        s[0] = own[i]
        s[1] = other[0, i]
        s[2] = far[0, i]
        s[3] = far[1, i]


def query_pairs_kernel(own, next_, other, g, n):
    g[0] = own[...]
    g[1] = other[0]
    n[0] = next_[...]
    n[1] = other[1]


def back_kernel(g, y, z, d, _, out):
    for j, r in enumerate((g, z, y, d)):
        out[j] = r[1]


def project(code, xs, w):
    acc = jnp.zeros((ROWS, COLS), F32)
    for j in range(4):
        rows = pl.ds(pl.multiple_of(rank_of(code, j) * PART, PART), PART)
        acc += jnp.dot(xs[j], w[rows, :], preferred_element_type=F32)
    return acc


def head_norm(v, gain):
    return v * lax.rsqrt(jnp.mean(v * v, axis=-1, keepdims=True) + 1e-06) * gain


def query_kernel(idx, x0, x1, x2, x3, m2, wq, qg, own, next_, other, qa, xs):
    blocks = (x0, x1, x2, x3)
    total = sum(jnp.sum(b[:ROWS].astype(F32), axis=-1, keepdims=True) for b in blocks)
    mean = total / WIDTH
    square = jnp.zeros_like(mean)
    for b in blocks:
        centred = b[:ROWS].astype(F32) - mean
        square += jnp.sum(centred * centred, axis=-1, keepdims=True)
    rstd = lax.rsqrt(square / WIDTH + 1e-06)
    for j, b in enumerate(blocks):
        mods = (m2[...] if j == 2 else b[ROWS : ROWS + 16]).astype(F32)
        for i in range(IMG):
            rows = slice(i * TOK, (i + 1) * TOK)
            normed = (b[rows].astype(F32) - mean[rows]) * rstd[rows]
            out = normed * (1.0 + mods[IMG + i : IMG + i + 1, :]) + mods[i : i + 1, :]
            xs[j, rows, :] = out.astype(BF16)
    acc = project(idx, xs, wq)
    for h in range(4):
        cut = slice(h * HEAD, (h + 1) * HEAD)
        qa[:, cut] = head_norm(acc[:, cut], qg[:1]).astype(BF16)
    own[...] = qa[:, head_slice(idx, 0)]
    next_[...] = qa[:, head_slice(idx, 1)]
    for j in range(2):
        other[j] = qa[:, head_slice(idx, 2 + j)]


def project_queries(idx, xs, wq, gain):
    return pl.pallas_call(
        query_kernel,
        out_shape=[
            jax.ShapeDtypeStruct((ROWS, HEAD), BF16),
            jax.ShapeDtypeStruct((ROWS, HEAD), BF16),
            jax.ShapeDtypeStruct((2, ROWS, HEAD), BF16),
            jax.ShapeDtypeStruct((ROWS, COLS), BF16),
            jax.ShapeDtypeStruct((4, ROWS, PART), BF16),
        ],
        in_specs=[smem()] + vmem(7),
        out_specs=vmem(5),
        compiler_params=params(16),
        cost_estimate=pl.CostEstimate(
            flops=2 * ROWS * WIDTH * COLS, bytes_accessed=5 << 20, transcendentals=0
        ),
        name="queries",
    )(idx, *xs, wq, gain)


def fresh_kernel(idx, xs, qa, wk, wv, kg, _, fk, fv, out, lse):
    acc = project(idx, xs, wk)
    for h in range(4):
        cut = slice(h * HEAD, (h + 1) * HEAD)
        fk[:, cut] = head_norm(acc[:, cut], kg[1:]).astype(BF16)
    fv[...] = project(idx, xs, wv).astype(BF16)
    shape = (ROWS, ROWS)
    row_image = lax.broadcasted_iota(jnp.int32, shape, 0) // TOK
    col_image = lax.broadcasted_iota(jnp.int32, shape, 1) // TOK
    lanes = lax.broadcasted_iota(jnp.int32, (ROWS, HEAD), 1)
    levels = jnp.zeros((ROWS, HEAD), F32)
    for h in range(4):
        cut = slice(h * HEAD, (h + 1) * HEAD)
        s = dot_t(qa[:, cut], fk[:, cut]) * SCORE
        s = jnp.where(row_image == col_image, s, -1e30)
        top = jnp.max(s, axis=-1, keepdims=True)
        p = jnp.exp2(s - top)
        total = jnp.sum(p, axis=-1, keepdims=True)
        numer = jnp.dot(p.astype(BF16), fv[:, cut], preferred_element_type=F32)
        out[:, cut] = numer / total
        levels = jnp.where(lanes == h, top + jnp.log2(total), levels)
    lse[...] = levels


def fresh(idx, xs, qa, wk, wv, gain, dep):
    return pl.pallas_call(
        fresh_kernel,
        out_shape=[jax.ShapeDtypeStruct((ROWS, COLS), BF16)] * 2
        + [
            jax.ShapeDtypeStruct((ROWS, COLS), F32),
            jax.ShapeDtypeStruct((ROWS, HEAD), F32),
        ],
        in_specs=[smem()] + vmem(5) + anywhere(1),
        out_specs=vmem(4),
        compiler_params=params(16),
        cost_estimate=pl.CostEstimate(
            flops=4 * ROWS * WIDTH * COLS, bytes_accessed=9 << 20, transcendentals=0
        ),
        name="fresh",
    )(idx, xs, qa, wk, wv, gain, dep)


def attend_part(q, stream, state, mask):
    entries = 16
    count = entries * TOK
    for c in range(stream.shape[0] // entries):
        span = slice(c * entries, (c + 1) * entries)
        k = stream[span, 0].reshape(count, HEAD)
        v = stream[span, 1].reshape(count, HEAD)
        s = dot_t(q, k) * SCORE
        if state is None:
            s = jnp.concatenate(
                [jnp.where(mask, -1e30, s[:, : 4 * TOK]), s[:, 4 * TOK :]], axis=1
            )
            top = jnp.max(s, axis=-1, keepdims=True)
            p = jnp.exp2(s - top)
            total = jnp.sum(p, axis=-1, keepdims=True)
            numer = jnp.dot(p.astype(BF16), v, preferred_element_type=F32)
        else:
            old, total, numer = state
            top = jnp.maximum(old, jnp.max(s, axis=-1, keepdims=True))
            factor = jnp.exp2(old - top)
            p = jnp.exp2(s - top)
            total = total * factor + jnp.sum(p, axis=-1, keepdims=True)
            numer = numer * factor + jnp.dot(p.astype(BF16), v, preferred_element_type=F32)
        state = (top, total, numer)
    return state


def attend_kernel(number, first_patch, *refs):
    groups, (s0, t0, s1, t1) = refs[:number], refs[number : number + 4]
    outs = refs[-number:]
    count = 2 * len(groups)
    shape = (count * TOK, 4 * TOK)
    row_patch = lax.broadcasted_iota(jnp.int32, shape, 0) // TOK + first_patch
    col_patch = lax.broadcasted_iota(jnp.int32, shape, 1) // TOK
    lse_rows = [jnp.zeros((1, HEAD), F32) for _ in range(count)]
    row = lax.broadcasted_iota(jnp.int32, (TOK, HEAD), 0)
    lane = lax.broadcasted_iota(jnp.int32, (TOK, HEAD), 1)
    for i, streams in enumerate(((s0, t0), (s1, t1))):
        q = jnp.concatenate(
            [r[j, i * TOK : (i + 1) * TOK] for r in groups for j in range(2)], axis=0
        )
        state = None
        for stream in streams:
            state = attend_part(q, stream, state, row_patch == col_patch)
        top, total, numer = state
        out = (numer / total).astype(BF16)
        level = top + jnp.log2(total)
        for d in range(count):
            span = slice(d * TOK, (d + 1) * TOK)
            outs[d // 2][d % 2, i * TOK : (i + 1) * TOK, :] = out[span]
            lse_rows[d] += jnp.sum(
                jnp.where(lane == row + i * TOK, level[span], 0.0), axis=0, keepdims=True
            )
    sub = lax.broadcasted_iota(jnp.int32, (16, HEAD), 0)
    for d in range(count):
        high = lse_rows[d].astype(BF16).astype(F32)
        rest = lse_rows[d] - high
        middle = rest.astype(BF16).astype(F32)
        low = rest - middle
        tail = jnp.where(sub == 0, high, jnp.where(sub == 1, middle, jnp.where(sub == 2, low, 0.0)))
        outs[d // 2][d % 2, ROWS : ROWS + 16, :] = tail.astype(BF16)


def attend(groups, streams, first_patch, deps=()):
    number = len(groups)
    return pl.pallas_call(
        functools.partial(attend_kernel, number, first_patch),
        out_shape=[jax.ShapeDtypeStruct((2, ROWS + 16, HEAD), BF16)] * number,
        in_specs=vmem(number + 4) + anywhere(len(deps)),
        out_specs=vmem(number),
        compiler_params=params(32),
        cost_estimate=pl.CostEstimate(
            flops=2 * number << 30, bytes_accessed=8 << 20, transcendentals=1 << 22
        ),
        name="attend",
    )(*groups, *streams, *deps)


def combine_kernel(heads, g, z, y, d, other, near_out, near_lse, att):
    row = lax.broadcasted_iota(jnp.int32, (ROWS, HEAD), 0)
    lane = lax.broadcasted_iota(jnp.int32, (ROWS, HEAD), 1)
    halves = ((g.at[0], z.at[0]), (y.at[0], d.at[0]), (other.at[0], other.at[1]),
              (other.at[2], other.at[3]))
    for h, pair in enumerate(halves):
        cut = head_slice(heads, h)
        levels = [
            jnp.sum(jnp.where(lane == head_of(heads, h), near_lse[...], 0.0), axis=1, keepdims=True)
        ]
        parts = [near_out[:, cut]]
        for r in pair:
            tail = r[ROWS : ROWS + 16, :].astype(F32)
            level = tail[0:1] + tail[1:2] + tail[2:3]
            levels.append(jnp.sum(jnp.where(lane == row, level, 0.0), axis=1, keepdims=True))
            parts.append(r[:ROWS, :].astype(F32))
        top = jnp.maximum(jnp.maximum(levels[0], levels[1]), levels[2])
        weights = [jnp.exp2(level - top) for level in levels]
        out = sum(w * p for w, p in zip(weights, parts))
        att[:, cut] = (out / sum(weights)).astype(BF16)


def combine(heads, parts, near_out, near_lse):
    return pl.pallas_call(
        combine_kernel,
        out_shape=jax.ShapeDtypeStruct((ROWS, COLS), BF16),
        in_specs=[smem()] + vmem(7),
        out_specs=pl.BlockSpec(memory_space=pltpu.VMEM),
        compiler_params=params(8),
        name="combine",
    )(heads, *parts, near_out, near_lse)


def swap(value, axis, step):
    flips = ((1, 3), (3, 1))[step]
    if axis == "zh":
        names, far, near_ = ("core", axis), 1, 4
    else:
        names, far, near_ = (axis, "core"), 2, 1
    perm = [
        (a * far + c * near_, (a ^ flips[c]) * far + c * near_)
        for a in range(4)
        for c in range(2)
    ]
    return lax.ppermute(value, names, perm)


def diagonal(value):
    perm = [
        (z * 8 + y * 2 + c, (z ^ 1) * 8 + (y ^ (1, 3)[c]) * 2 + c)
        for z in range(2)
        for y in range(4)
        for c in range(2)
    ]
    return lax.ppermute(value, ("zl", "y", "core"), perm)


def on_device(activations, mod_shift, mod_scale, w_query, w_key, w_value,
              query_gain, key_gain, stale_keys, stale_values):
    code = lax.axis_index("zh") * 8 + lax.axis_index("y") * 2 + lax.axis_index("core")
    code = code.astype(jnp.int32).reshape(1)

    own, next_, other, x0 = pack(
        code, stale_keys, stale_values, activations.reshape(ROWS, PART), mod_shift, mod_scale
    )
    x1 = swap(x0, "zh", 0)
    x2 = swap(activations.reshape(ROWS, PART), "zh", 1)
    other = lax.ppermute(other, "core", FLIP)
    shape = (IMG, 2, TOK, HEAD)
    (far,) = call(pair_kernel, "pair", 8, [(2,) + shape], (next_, other))
    far = swap(far, "y", 0)
    gains = (query_gain.reshape(1, HEAD), key_gain.reshape(1, HEAD))
    x0, own, gains = hold(x0, own, gains)
    s0, s1 = call(
        stack_kernel, "stack", 8, [(4,) + shape[1:]] * 2, (own, other, far), (gains,)
    )
    s0, s1 = join([(s0, swap(s0, "y", 1)), (s1, swap(s1, "x", 0))], (x1, x2))
    x3 = swap(x1, "zh", 1)
    cost = pl.CostEstimate(flops=8 << 30, bytes_accessed=1 << 20, transcendentals=0)
    (m2,) = call(mods_kernel, "mods", 8, [(16, PART)], (x1,), (), cost)
    m2 = lax.ppermute(m2, "core", FLIP)
    own, next_, other, qa, xs = project_queries(
        code, (x0, x1, x2, x3, m2), w_query, gains
    )
    s0, s1 = join([(s0, swap(s0, "x", 0)), (s1, swap(s1, "x", 1))], (own,))
    t0, t1 = swap(s0, "x", 1), swap(s1, "y", 1)

    other = lax.ppermute(other, "core", FLIP)
    cost = pl.CostEstimate(flops=8 << 30, bytes_accessed=1 << 20, transcendentals=0)
    g, n = call(
        query_pairs_kernel, "query_pairs", 8, [(2, ROWS, HEAD)] * 2, (own, next_, other), (), cost
    )
    groups = (swap(n, "y", 0), lax.ppermute(g, "zl", FLIP), diagonal(n))
    streams = (s0, t0, s1, t1)
    fk, fv, near_out, near_lse = fresh(code, xs, qa, w_key, w_value, gains, g)
    py, pz, pd = attend(groups, streams, 2, (near_lse,))
    (pg,) = attend((g,), streams, 0, (py,))
    py, pz, pd = swap(py, "y", 0), lax.ppermute(pz, "zl", FLIP), diagonal(pd)
    (back,) = call(
        back_kernel, "back", 8, [(4, ROWS + 16, HEAD)], (pg, py, pz, pd), (mark(pd),)
    )
    back = lax.ppermute(back, "core", FLIP)
    att = combine(code, (pg, pz, py, pd, back), near_out, near_lse)
    shape = (IMG, TOK, COLS)
    return att.reshape(shape), fk.reshape(shape), fv.reshape(shape)


def solution(mesh):
    split = Mesh(mesh.devices.reshape(4, 2, 4, 2, 4), ("x", "zl", "y", "core", "zh"))
    patch = ("x", "zl", "y", "core")
    rows = P(None, patch, "zh")
    cols = P(None, "zh")
    return jax.shard_map(
        on_device,
        mesh=split,
        in_specs=(rows, cols, cols, cols, cols, cols, P(), P(), rows, rows),
        out_specs=(rows, rows, rows),
        check_vma=False,
    )
```

```python
import functools
import math

import jax
import jax.numpy as jnp
from jax import lax
from jax.experimental import pallas as pl
from jax.experimental.pallas import tpu as pltpu
from jax.sharding import Mesh, PartitionSpec as P

HEAD = 128
TOK = 64
IMG = 2
WIDTH = 4096
PART = 1024
COLS = 512
ROWS = IMG * TOK
SCORE = math.log2(math.e) / math.sqrt(HEAD)
F32 = jnp.float32
BF16 = jnp.bfloat16
FLIP = [(0, 1), (1, 0)]


def params(limit):
    return pltpu.CompilerParams(vmem_limit_bytes=limit * 1024 * 1024)


def vmem(count):
    return [pl.BlockSpec(memory_space=pltpu.VMEM)] * count


def hbm(count):
    return [pl.BlockSpec(memory_space=pltpu.HBM)] * count


def anywhere(count):
    return [pl.BlockSpec(memory_space=pl.ANY)] * count


def smem():
    return pl.BlockSpec(memory_space=pltpu.SMEM)


def dot_t(a, b):
    return lax.dot_general(a, b, (((1,), (1,)), ((), ())), preferred_element_type=F32)


def head_of(code, d):
    core, y = code[0] & 1, (code[0] >> 1) & 3
    side = core ^ (d >> 1)
    bit = jnp.where(side == 0, (y ^ (y >> 1)) & 1, y >> 1)
    return 2 * side + (bit ^ (d & 1))


def head_slice(code, d):
    return pl.ds(pl.multiple_of(head_of(code, d) * HEAD, HEAD), HEAD)


def rank_of(code, j):
    flips = (0, jnp.where(code[0] & 1 == 0, 1, 3), jnp.where(code[0] & 1 == 0, 3, 1), 2)
    return (code[0] >> 3) ^ flips[j]


def pack_kernel(heads, keys, values, x, shift, scale, own, next_, other, pay, mods, sems):
    copies = []

    def copy(source, target):
        copies.append(pltpu.make_async_copy(source, target, sems.at[len(copies)]))
        copies[-1].start()

    copy(shift, mods.at[0])
    copy(scale, mods.at[1])
    copy(x, pay.at[:ROWS])
    for d, out in ((2, other.at[0]), (3, other.at[1]), (1, next_), (0, own)):
        cut = head_slice(heads, d)
        for i in range(IMG):
            for j, source in enumerate((keys, values)):
                copy(source.at[i, :, cut], out.at[i, j])
    for one in copies[:2]:
        one.wait()
    pay[ROWS:] = jnp.zeros((16, PART), BF16)
    pay[ROWS : ROWS + IMG] = mods[0]
    pay[ROWS + IMG : ROWS + 2 * IMG] = mods[1]
    for one in copies[2:]:
        one.wait()


def pack(heads, keys, values, x, shift, scale):
    shape = (IMG, 2, TOK, HEAD)
    return pl.pallas_call(
        pack_kernel,
        out_shape=[
            jax.ShapeDtypeStruct(shape, BF16),
            jax.ShapeDtypeStruct(shape, BF16),
            jax.ShapeDtypeStruct((2,) + shape, BF16),
            jax.ShapeDtypeStruct((ROWS + 16, PART), BF16),
        ],
        in_specs=[smem()] + hbm(5),
        out_specs=vmem(4),
        scratch_shapes=[pltpu.VMEM((2, IMG, PART), BF16), pltpu.SemaphoreType.DMA((19,))],
        compiler_params=params(56),
        name="pack",
    )(heads, keys, values, x, shift, scale)


def call(kernel, name, limit, shapes, operands, deps=(), cost=None):
    return pl.pallas_call(
        kernel,
        out_shape=[jax.ShapeDtypeStruct(s, BF16) for s in shapes],
        in_specs=vmem(len(operands)) + anywhere(len(deps)),
        out_specs=vmem(len(shapes)),
        compiler_params=params(limit),
        cost_estimate=cost,
        name=name,
    )(*operands, *deps)


def join(groups, deps=()):
    counts = [len(g) for g in groups]

    def kernel(*refs):
        ins, outs = refs[: sum(counts)], refs[sum(counts) + len(deps) :]
        at = 0
        for out, count in zip(outs, counts):
            row = 0
            for r in ins[at : at + count]:
                out[row : row + r.shape[0]] = r[...]
                row += r.shape[0]
            at += count

    def shape(group):
        rows = sum(v.shape[0] for v in group)
        return jax.ShapeDtypeStruct((rows,) + group[0].shape[1:], group[0].dtype)

    return pl.pallas_call(
        kernel,
        out_shape=[shape(g) for g in groups],
        in_specs=vmem(sum(counts)) + anywhere(len(deps)),
        out_specs=vmem(len(groups)),
        compiler_params=params(12),
        name="join",
    )(*[v for g in groups for v in g], *deps)


def hold(x0, own, gains):
    def kernel(x_in, own_in, qg, kg, x_out, own_out, gains_out):
        x_out[...] = x_in[...]
        own_out[...] = own_in[...]
        gains_out[:1] = qg[...]
        gains_out[1:] = kg[...]

    return pl.pallas_call(
        kernel,
        out_shape=[
            jax.ShapeDtypeStruct(x0.shape, BF16),
            jax.ShapeDtypeStruct(own.shape, BF16),
            jax.ShapeDtypeStruct((2, HEAD), F32),
        ],
        in_specs=vmem(4),
        out_specs=vmem(3),
        compiler_params=params(8),
        cost_estimate=pl.CostEstimate(flops=0, bytes_accessed=32 << 20, transcendentals=0),
        name="hold",
    )(x0, own, *gains)


def mark(dep):
    def kernel(_, out):
        out[...] = jnp.zeros_like(out)

    return pl.pallas_call(
        kernel,
        out_shape=jax.ShapeDtypeStruct((8, HEAD), F32),
        in_specs=anywhere(1),
        out_specs=pl.BlockSpec(memory_space=pltpu.VMEM),
        compiler_params=params(4),
        cost_estimate=pl.CostEstimate(flops=4 << 30, bytes_accessed=4096, transcendentals=0),
        name="mark",
    )(dep)


def mods_kernel(x, out):
    out[...] = x[ROWS:]


def pair_kernel(a, b, out):
    out[0] = a[...]
    out[1] = b[1]


def stack_kernel(own, other, far, _, s0, s1):
    for i, s in enumerate((s0, s1)):
        s[0] = own[i]
        s[1] = other[0, i]
        s[2] = far[0, i]
        s[3] = far[1, i]


def query_pairs_kernel(own, next_, other, g, n):
    g[0] = own[...]
    g[1] = other[0]
    n[0] = next_[...]
    n[1] = other[1]


def back_kernel(g, y, z, d, _, out, kept):
    for j, r in enumerate((g, z, y, d)):
        out[j] = r[1]
        kept[j] = r[0]


def project(code, xs, w):
    acc = jnp.zeros((ROWS, COLS), F32)
    for j in range(4):
        rows = pl.ds(pl.multiple_of(rank_of(code, j) * PART, PART), PART)
        acc += jnp.dot(xs[j], w[rows, :], preferred_element_type=F32)
    return acc


def head_norm(v, gain):
    return v * lax.rsqrt(jnp.mean(v * v, axis=-1, keepdims=True) + 1e-06) * gain


def query_kernel(idx, x0, x1, x2, x3, m2, wq, qg, own, next_, other, qa, xs):
    blocks = (x0, x1, x2, x3)
    total = sum(jnp.sum(b[:ROWS].astype(F32), axis=-1, keepdims=True) for b in blocks)
    mean = total / WIDTH
    square = jnp.zeros_like(mean)
    for b in blocks:
        centred = b[:ROWS].astype(F32) - mean
        square += jnp.sum(centred * centred, axis=-1, keepdims=True)
    rstd = lax.rsqrt(square / WIDTH + 1e-06)
    for j, b in enumerate(blocks):
        mods = (m2[...] if j == 2 else b[ROWS : ROWS + 16]).astype(F32)
        for i in range(IMG):
            rows = slice(i * TOK, (i + 1) * TOK)
            normed = (b[rows].astype(F32) - mean[rows]) * rstd[rows]
            out = normed * (1.0 + mods[IMG + i : IMG + i + 1, :]) + mods[i : i + 1, :]
            xs[j, rows, :] = out.astype(BF16)
    acc = project(idx, xs, wq)
    for h in range(4):
        cut = slice(h * HEAD, (h + 1) * HEAD)
        qa[:, cut] = head_norm(acc[:, cut], qg[:1]).astype(BF16)
    own[...] = qa[:, head_slice(idx, 0)]
    next_[...] = qa[:, head_slice(idx, 1)]
    for j in range(2):
        other[j] = qa[:, head_slice(idx, 2 + j)]


def project_queries(idx, xs, wq, gain):
    return pl.pallas_call(
        query_kernel,
        out_shape=[
            jax.ShapeDtypeStruct((ROWS, HEAD), BF16),
            jax.ShapeDtypeStruct((ROWS, HEAD), BF16),
            jax.ShapeDtypeStruct((2, ROWS, HEAD), BF16),
            jax.ShapeDtypeStruct((ROWS, COLS), BF16),
            jax.ShapeDtypeStruct((4, ROWS, PART), BF16),
        ],
        in_specs=[smem()] + vmem(7),
        out_specs=vmem(5),
        compiler_params=params(16),
        cost_estimate=pl.CostEstimate(
            flops=2 * ROWS * WIDTH * COLS, bytes_accessed=5 << 20, transcendentals=0
        ),
        name="queries",
    )(idx, *xs, wq, gain)


def fresh_kernel(idx, xs, qa, wk, wv, kg, _, fk, fv, out, lse):
    acc = project(idx, xs, wk)
    for h in range(4):
        cut = slice(h * HEAD, (h + 1) * HEAD)
        fk[:, cut] = head_norm(acc[:, cut], kg[1:]).astype(BF16)
    fv[...] = project(idx, xs, wv).astype(BF16)
    shape = (ROWS, ROWS)
    row_image = lax.broadcasted_iota(jnp.int32, shape, 0) // TOK
    col_image = lax.broadcasted_iota(jnp.int32, shape, 1) // TOK
    lanes = lax.broadcasted_iota(jnp.int32, (ROWS, HEAD), 1)
    levels = jnp.zeros((ROWS, HEAD), F32)
    for h in range(4):
        cut = slice(h * HEAD, (h + 1) * HEAD)
        s = dot_t(qa[:, cut], fk[:, cut]) * SCORE
        s = jnp.where(row_image == col_image, s, -1e30)
        top = jnp.max(s, axis=-1, keepdims=True)
        p = jnp.exp2(s - top)
        total = jnp.sum(p, axis=-1, keepdims=True)
        numer = jnp.dot(p.astype(BF16), fv[:, cut], preferred_element_type=F32)
        out[:, cut] = numer / total
        levels = jnp.where(lanes == h, top + jnp.log2(total), levels)
    lse[...] = levels


def fresh(idx, xs, qa, wk, wv, gain, dep):
    return pl.pallas_call(
        fresh_kernel,
        out_shape=[jax.ShapeDtypeStruct((ROWS, COLS), BF16)] * 2
        + [
            jax.ShapeDtypeStruct((ROWS, COLS), F32),
            jax.ShapeDtypeStruct((ROWS, HEAD), F32),
        ],
        in_specs=[smem()] + vmem(5) + anywhere(1),
        out_specs=vmem(4),
        compiler_params=params(16),
        cost_estimate=pl.CostEstimate(
            flops=4 * ROWS * WIDTH * COLS, bytes_accessed=9 << 20, transcendentals=0
        ),
        name="fresh",
    )(idx, xs, qa, wk, wv, gain, dep)


def attend_part(q, stream, state, mask):
    entries = 16
    count = entries * TOK
    for c in range(stream.shape[0] // entries):
        span = slice(c * entries, (c + 1) * entries)
        k = stream[span, 0].reshape(count, HEAD)
        v = stream[span, 1].reshape(count, HEAD)
        s = dot_t(q, k) * SCORE
        if state is None:
            s = jnp.concatenate(
                [jnp.where(mask, -1e30, s[:, : 4 * TOK]), s[:, 4 * TOK :]], axis=1
            )
            top = jnp.max(s, axis=-1, keepdims=True)
            p = jnp.exp2(s - top)
            total = jnp.sum(p, axis=-1, keepdims=True)
            numer = jnp.dot(p.astype(BF16), v, preferred_element_type=F32)
        else:
            old, total, numer = state
            top = jnp.maximum(old, jnp.max(s, axis=-1, keepdims=True))
            factor = jnp.exp2(old - top)
            p = jnp.exp2(s - top)
            total = total * factor + jnp.sum(p, axis=-1, keepdims=True)
            numer = numer * factor + jnp.dot(p.astype(BF16), v, preferred_element_type=F32)
        state = (top, total, numer)
    return state


def attend_kernel(number, first_patch, *refs):
    groups, (s0, t0, s1, t1) = refs[:number], refs[number : number + 4]
    outs = refs[-number:]
    count = 2 * len(groups)
    shape = (count * TOK, 4 * TOK)
    row_patch = lax.broadcasted_iota(jnp.int32, shape, 0) // TOK + first_patch
    col_patch = lax.broadcasted_iota(jnp.int32, shape, 1) // TOK
    lse_rows = [jnp.zeros((1, HEAD), F32) for _ in range(count)]
    row = lax.broadcasted_iota(jnp.int32, (TOK, HEAD), 0)
    lane = lax.broadcasted_iota(jnp.int32, (TOK, HEAD), 1)
    for i, streams in enumerate(((s0, t0), (s1, t1))):
        q = jnp.concatenate(
            [r[j, i * TOK : (i + 1) * TOK] for r in groups for j in range(2)], axis=0
        )
        state = None
        for stream in streams:
            state = attend_part(q, stream, state, row_patch == col_patch)
        top, total, numer = state
        out = (numer / total).astype(BF16)
        level = top + jnp.log2(total)
        for d in range(count):
            span = slice(d * TOK, (d + 1) * TOK)
            outs[d // 2][d % 2, i * TOK : (i + 1) * TOK, :] = out[span]
            lse_rows[d] += jnp.sum(
                jnp.where(lane == row + i * TOK, level[span], 0.0), axis=0, keepdims=True
            )
    sub = lax.broadcasted_iota(jnp.int32, (16, HEAD), 0)
    for d in range(count):
        high = lse_rows[d].astype(BF16).astype(F32)
        rest = lse_rows[d] - high
        middle = rest.astype(BF16).astype(F32)
        low = rest - middle
        tail = jnp.where(sub == 0, high, jnp.where(sub == 1, middle, jnp.where(sub == 2, low, 0.0)))
        outs[d // 2][d % 2, ROWS : ROWS + 16, :] = tail.astype(BF16)


def attend(groups, streams, first_patch, deps=()):
    number = len(groups)
    return pl.pallas_call(
        functools.partial(attend_kernel, number, first_patch),
        out_shape=[jax.ShapeDtypeStruct((2, ROWS + 16, HEAD), BF16)] * number,
        in_specs=vmem(number + 4) + anywhere(len(deps)),
        out_specs=vmem(number),
        compiler_params=params(32),
        cost_estimate=pl.CostEstimate(
            flops=2 * number << 30, bytes_accessed=8 << 20, transcendentals=1 << 22
        ),
        name="attend",
    )(*groups, *streams, *deps)


def merge(code, head, pair, near_out, near_lse):
    row = lax.broadcasted_iota(jnp.int32, (ROWS, HEAD), 0)
    lane = lax.broadcasted_iota(jnp.int32, (ROWS, HEAD), 1)
    level = jnp.where(lane == head_of(code, head), near_lse[...], 0.0)
    levels = [jnp.sum(level, axis=1, keepdims=True)]
    parts = [near_out[:, head_slice(code, head)]]
    for r in pair:
        tail = r[ROWS : ROWS + 16, :].astype(F32)
        level = tail[0:1] + tail[1:2] + tail[2:3]
        levels.append(jnp.sum(jnp.where(lane == row, level, 0.0), axis=1, keepdims=True))
        parts.append(r[:ROWS, :].astype(F32))
    top = jnp.maximum(jnp.maximum(levels[0], levels[1]), levels[2])
    weights = [jnp.exp2(level - top) for level in levels]
    out = sum(w * p for w, p in zip(weights, parts))
    return (out / sum(weights)).astype(BF16)


def combine_here_kernel(code, kept, near_out, near_lse, out):
    for h in range(2):
        out[h] = merge(code, h, (kept.at[2 * h], kept.at[2 * h + 1]), near_out, near_lse)


def combine_here(code, kept, near_out, near_lse):
    return pl.pallas_call(
        combine_here_kernel,
        out_shape=jax.ShapeDtypeStruct((2, ROWS, HEAD), BF16),
        in_specs=[smem()] + vmem(3),
        out_specs=pl.BlockSpec(memory_space=pltpu.VMEM),
        compiler_params=params(8),
        name="combine_here",
    )(code, kept, near_out, near_lse)


def combine_kernel(code, other, here, near_out, near_lse, att):
    for h in range(2):
        att[:, head_slice(code, h)] = here[h]
        pair = (other.at[2 * h], other.at[2 * h + 1])
        att[:, head_slice(code, 2 + h)] = merge(code, 2 + h, pair, near_out, near_lse)


def combine(code, other, here, near_out, near_lse):
    return pl.pallas_call(
        combine_kernel,
        out_shape=jax.ShapeDtypeStruct((ROWS, COLS), BF16),
        in_specs=[smem()] + vmem(4),
        out_specs=pl.BlockSpec(memory_space=pltpu.VMEM),
        compiler_params=params(8),
        name="combine",
    )(code, other, here, near_out, near_lse)


def swap(value, axis, step):
    flips = ((1, 3), (3, 1))[step]
    if axis == "zh":
        names, far, near_ = ("core", axis), 1, 4
    else:
        names, far, near_ = (axis, "core"), 2, 1
    perm = [
        (a * far + c * near_, (a ^ flips[c]) * far + c * near_)
        for a in range(4)
        for c in range(2)
    ]
    return lax.ppermute(value, names, perm)


def diagonal(value):
    perm = [
        (z * 8 + y * 2 + c, (z ^ 1) * 8 + (y ^ (1, 3)[c]) * 2 + c)
        for z in range(2)
        for y in range(4)
        for c in range(2)
    ]
    return lax.ppermute(value, ("zl", "y", "core"), perm)


def on_device(activations, mod_shift, mod_scale, w_query, w_key, w_value,
              query_gain, key_gain, stale_keys, stale_values):
    code = lax.axis_index("zh") * 8 + lax.axis_index("y") * 2 + lax.axis_index("core")
    code = code.astype(jnp.int32).reshape(1)

    own, next_, other, x0 = pack(
        code, stale_keys, stale_values, activations.reshape(ROWS, PART), mod_shift, mod_scale
    )
    x1 = swap(x0, "zh", 0)
    x2 = swap(activations.reshape(ROWS, PART), "zh", 1)
    other = lax.ppermute(other, "core", FLIP)
    shape = (IMG, 2, TOK, HEAD)
    (far,) = call(pair_kernel, "pair", 8, [(2,) + shape], (next_, other))
    far = swap(far, "y", 0)
    gains = (query_gain.reshape(1, HEAD), key_gain.reshape(1, HEAD))
    x0, own, gains = hold(x0, own, gains)
    s0, s1 = call(
        stack_kernel, "stack", 8, [(4,) + shape[1:]] * 2, (own, other, far), (gains,)
    )
    s0, s1 = join([(s0, swap(s0, "y", 1)), (s1, swap(s1, "x", 0))], (x1, x2))
    x3 = swap(x1, "zh", 1)
    cost = pl.CostEstimate(flops=8 << 30, bytes_accessed=1 << 20, transcendentals=0)
    (m2,) = call(mods_kernel, "mods", 8, [(16, PART)], (x1,), (), cost)
    m2 = lax.ppermute(m2, "core", FLIP)
    own, next_, other, qa, xs = project_queries(
        code, (x0, x1, x2, x3, m2), w_query, gains
    )
    s0, s1 = join([(s0, swap(s0, "x", 0)), (s1, swap(s1, "x", 1))], (own,))
    t0, t1 = swap(s0, "x", 1), swap(s1, "y", 1)

    other = lax.ppermute(other, "core", FLIP)
    cost = pl.CostEstimate(flops=8 << 30, bytes_accessed=1 << 20, transcendentals=0)
    g, n = call(
        query_pairs_kernel, "query_pairs", 8, [(2, ROWS, HEAD)] * 2, (own, next_, other), (), cost
    )
    groups = (swap(n, "y", 0), lax.ppermute(g, "zl", FLIP), diagonal(n))
    streams = (s0, t0, s1, t1)
    fk, fv, near_out, near_lse = fresh(code, xs, qa, w_key, w_value, gains, g)
    py, pz, pd = attend(groups, streams, 2, (near_lse,))
    (pg,) = attend((g,), streams, 0, (py,))
    py, pz, pd = swap(py, "y", 0), lax.ppermute(pz, "zl", FLIP), diagonal(pd)
    back, kept = call(
        back_kernel, "back", 8, [(4, ROWS + 16, HEAD)] * 2, (pg, py, pz, pd), (mark(pd),)
    )
    back = lax.ppermute(back, "core", FLIP)
    here = combine_here(code, kept, near_out, near_lse)
    att = combine(code, back, here, near_out, near_lse)
    shape = (IMG, TOK, COLS)
    return att.reshape(shape), fk.reshape(shape), fv.reshape(shape)


def solution(mesh):
    split = Mesh(mesh.devices.reshape(4, 2, 4, 2, 4), ("x", "zl", "y", "core", "zh"))
    patch = ("x", "zl", "y", "core")
    rows = P(None, patch, "zh")
    cols = P(None, "zh")
    return jax.shard_map(
        on_device,
        mesh=split,
        in_specs=(rows, cols, cols, cols, cols, cols, P(), P(), rows, rows),
        out_specs=(rows, rows, rows),
        check_vma=False,
    )
```
